768 devices in a mesh: nodes: 16 (over y, x_lo), feat: 48 (over x_hi, z, core).
Axes of the slice: x: 4 (x_hi: 2, x_lo: 2; x = x_hi * 2 + x_lo), y: 8, z: 12, core: 2. Of those that a mesh axis runs over, the one named last changes fastest.
Arguments:
- features: bfloat16 [98304, 256], P(('feat', 'nodes')), may hold values from -6 to 6
- weight: bfloat16 [256, 256], replicated, may hold values from -0.375 to 0.375
- tiles: bfloat16 [36864, 128, 128], P(('nodes', 'feat')), may hold values from -0.078125 to 0.078125
- tile_rows: int32 [36864], P(('nodes', 'feat')), may hold values from 0 to 47
- tile_cols: int32 [36864], P(('nodes', 'feat')), may hold values from 0 to 15
- live: int32 [768], P(('nodes', 'feat')), may hold values from 24 to 48, as said below
- cotangent: bfloat16 [98304, 256], P(('nodes', 'feat')), may hold values from -6 to 6
Outputs:
- output: bfloat16 [98304, 256], P(('nodes', 'feat'))
- feature_grad: bfloat16 [98304, 256], P(('feat', 'nodes'))
- weight_grad: float32 [256, 256], replicated
The draws below stay inside these ranges and needn't reach their ends.
Inputs may be any that keep to these rules, and one draw needn't show every extreme that they name: `live`: some block uses all 48 slots.
All inputs are finite; a program needn't handle non-finite values.
Results may differ from the reference program's by a relative error of at most 0.0049.
Values may be sent and summed in bfloat16 or wider, within the bound.
A program may use at most 64 MiB of HBM per device.

```python
import math
import jax
import jax.numpy as jnp
from jax import lax

F = 256
TILE = 128
ROWS_DEV = 128
TILE_DEV = 48
NODES = 98304
TILES = 36864
N_NODES = 16
N_FEAT = 48


def draw_live(key, part):
    key = jax.random.fold_in(key, 7)
    first_key, second_key = jax.random.split(key)
    block_count = N_NODES * N_FEAT
    counts = jax.random.randint(first_key, (block_count,), max(1, TILE_DEV // 2), TILE_DEV + 1, dtype=jnp.int32)
    position = jax.random.randint(second_key, (), 0, block_count, dtype=jnp.int32)
    counts = counts.at[position].set(TILE_DEV)
    return counts.astype(jnp.int32)


def with_ends(drawn, key, least, top_value):
    longest = drawn.shape.index(max(drawn.shape))
    spots = []
    for shift in (0, 1):
        where = [jax.random.randint(jax.random.fold_in(key, axis), (), 0, length) for axis, length in enumerate(drawn.shape)]
        where[longest] = (where[longest] + shift) % drawn.shape[longest]
        spots.append(tuple(where))
    return drawn.at[spots[0]].set(least).at[spots[1]].set(top_value)


def block_scale(stream_key, dims, pieces, smallest, largest):
    gain, own = 1.0, jax.random.fold_in(stream_key, 6)
    for dim, shards_of in pieces:
        draws = jnp.exp(jax.random.uniform(jax.random.fold_in(own, dim), (shards_of,), jnp.float32, smallest / len(pieces), largest / len(pieces)))
        gain = gain * jnp.repeat(draws, dims[dim] // shards_of).reshape([-1 if axis == dim else 1 for axis in range(len(dims))])
    return gain


def centred(key, extent, spread, limit, pieces=(), kind=jnp.bfloat16):
    result = jax.random.normal(key, extent, jnp.float32) * spread
    if len(pieces) > 0:
        result = block_scale(key, extent, pieces, -0.22, 0.18) * result
    return jnp.clip(result, min=-limit, max=limit).astype(kind)


def setup_inputs(seed: int = 0) -> dict:
    key_list = jax.random.split(jax.random.key(seed), 8)
    features = centred(key_list[0], (NODES, F), 1.0, 6.0, ((0, 768),))
    weight = centred(key_list[1], (F, F), F ** -0.5, 0.375)
    tiles = centred(key_list[2], (TILES, TILE, TILE), (TILE * TILE_DEV * TILE // ROWS_DEV) ** -0.5, 0.078125, ((0, 768),))
    tile_rows = with_ends(jax.random.randint(key_list[3], (TILES,), 0, ROWS_DEV * N_FEAT // TILE), jax.random.fold_in(key_list[3], 1), 0, (ROWS_DEV * N_FEAT // TILE) - 1).astype(jnp.int32)
    tile_cols = with_ends(jax.random.randint(key_list[4], (TILES,), 0, ROWS_DEV * N_NODES // TILE), jax.random.fold_in(key_list[4], 1), 0, (ROWS_DEV * N_NODES // TILE) - 1).astype(jnp.int32)
    live = draw_live(jax.random.fold_in(key_list[7], 71), 0)
    cotangent = centred(key_list[6], (NODES, F), 1.0, 6.0, ((0, 768),))
    return {"features": features, "weight": weight, "tiles": tiles, "tile_rows": tile_rows, "tile_cols": tile_cols, "live": live, "cotangent": cotangent}


def reference(features, weight, tiles, tile_rows, tile_cols, live, cotangent):
    feature_width = features.shape[1]
    nodes_total = features.shape[0]
    block_rows = ROWS_DEV * N_FEAT
    panel_width = ROWS_DEV * N_NODES
    block_count = N_NODES * N_FEAT
    tile_sets = tiles.reshape(block_count, TILE_DEV, TILE, TILE)
    row_sets = tile_rows.reshape(block_count, TILE_DEV)
    col_sets = tile_cols.reshape(block_count, TILE_DEV)
    offsets = jnp.arange(TILE, dtype=jnp.int32)
    block_ids = jnp.arange(block_count, dtype=jnp.int32)

    def indices(block_item):
        tile_set, row_set, col_set, live_count, block_index = block_item
        row_base = block_index // N_FEAT * block_rows
        col_base = block_index % N_FEAT * panel_width
        live_mask = (jnp.arange(TILE_DEV, dtype=jnp.int32) < live_count).astype(jnp.float32)
        row_index = (row_base + row_set[:, None] * TILE + offsets[None, :]).astype(jnp.int32)
        col_index = (col_base + col_set[:, None] * TILE + offsets[None, :]).astype(jnp.int32)
        return (tile_set, live_mask, row_index, col_index)

    def forward_step(summed, block_item):
        tile_set, live_mask, row_index, col_index = indices(block_item)
        pulled = features[col_index]
        products = jnp.einsum('kab,kbf->kaf', tile_set.astype(jnp.float32), pulled.astype(jnp.float32))
        products = products * live_mask[:, None, None]
        summed = summed.at[row_index.reshape(-1)].add(products.reshape(-1, feature_width))
        return (summed, None)
    items = (tile_sets, row_sets, col_sets, live, block_ids)
    summed, _ = lax.scan(forward_step, jnp.zeros((nodes_total, feature_width), jnp.float32), items)
    aggregate = summed.astype(jnp.bfloat16)
    output = jnp.dot(aggregate, weight, preferred_element_type=jnp.float32).astype(jnp.bfloat16)
    grad_agg = jnp.dot(cotangent, weight.T, preferred_element_type=jnp.float32).astype(jnp.bfloat16)

    def backward_step(summed_back, block_item):
        tile_set, live_mask, row_index, col_index = indices(block_item)
        pulled = grad_agg[row_index]
        back_terms = jnp.einsum('kab,kaf->kbf', tile_set.astype(jnp.float32), pulled.astype(jnp.float32))
        back_terms = back_terms * live_mask[:, None, None]
        summed_back = summed_back.at[col_index.reshape(-1)].add(back_terms.reshape(-1, feature_width))
        return (summed_back, None)
    summed_back, _ = lax.scan(backward_step, jnp.zeros((nodes_total, feature_width), jnp.float32), items)
    feature_grad = summed_back.astype(jnp.bfloat16)
    weight_grad = jnp.dot(aggregate.T, cotangent, preferred_element_type=jnp.float32) * (1.0 / math.sqrt(nodes_total))
    return (output, feature_grad, weight_grad)
```

```python
import functools
import math

import jax
import jax.numpy as jnp
from jax import lax
from jax.experimental import pallas as pl
from jax.experimental.pallas import tpu as pltpu
from jax.sharding import PartitionSpec as P

MESH = pl.DeviceIdType.MESH
VMEM = pl.BlockSpec(memory_space=pltpu.VMEM)
SMEM = pl.BlockSpec(memory_space=pltpu.SMEM)
LIMIT = 40 * 1024 * 1024
PAIR = 2


class Place:
    def __init__(self, n_nodes, n_feat):
        self.n_nodes, self.n_feat = n_nodes, n_feat
        self.ny, self.nz = n_nodes // PAIR, n_feat // (PAIR * PAIR)
        self.i, self.j = lax.axis_index("nodes"), lax.axis_index("feat")
        self.y, self.xl = lax.div(self.i, PAIR), lax.rem(self.i, PAIR)
        self.xh = lax.div(self.j, PAIR * self.nz)
        self.z = lax.rem(lax.div(self.j, PAIR), self.nz)
        self.core = lax.rem(self.j, PAIR)

    def node(self, y, xl):
        return y * PAIR + xl

    def feat(self, xh, z, core):
        return (xh * self.nz + z) * PAIR + core


def greet(partners):
    barrier = pltpu.get_barrier_semaphore()
    for device in partners:
        pl.semaphore_signal(barrier, inc=1, device_id=device, device_id_type=MESH)
    pl.semaphore_wait(barrier, len(partners))


def remote(src, dst, send_sem, recv_sem, device):
    return pltpu.make_async_remote_copy(
        src_ref=src, dst_ref=dst, send_sem=send_sem, recv_sem=recv_sem, device_id=device, device_id_type=MESH
    )


def gather_kernel(
    n_nodes, n_feat, x_ref, c_ref, x_all, c_all, xs, xr, zs, zr, cs, cr, ls, lr, ys, yr
):
    at = Place(n_nodes, n_feat)
    nz, ny = at.nz, at.ny
    z_near = [lax.rem(at.z + 1, nz), lax.rem(at.z + nz - 1, nz)]
    y_near = [lax.rem(at.y + 1, ny), lax.rem(at.y + ny - 1, ny)]
    sibling = (at.i, at.feat(at.xh, at.z, 1 - at.core))
    across = (at.i, at.feat(1 - at.xh, at.z, at.core))
    beside = (at.node(at.y, 1 - at.xl), at.j)
    along_z = [(at.i, at.feat(at.xh, z, at.core)) for z in z_near]
    along_y = [(at.node(y, at.xl), at.j) for y in y_near]
    greet([sibling, across, beside] + along_z + along_y)

    half_z, half_y = nz // 2, ny // 2

    def last_z(s, d):
        return half_z if s == d else nz - 1 - half_z

    def last_y(s, d):
        return half_y if s == d else ny - 1 - half_y

    def origin(place, count, d, t):
        return lax.rem(place + (count - t if d == 0 else t), count)

    def xh_of(s):
        return at.xh if s == 0 else 1 - at.xh

    def xl_of(s):
        return at.xl if s == 0 else 1 - at.xl

    def z_copy(s, d, t, origin_z):
        block = c_all.at[at.feat(xh_of(s), origin_z, at.core)]
        src = c_ref if (s == 0 and t == 1) else block
        return remote(src, block, zs.at[s, d, t - 1], zr.at[s, d, t - 1], along_z[d])

    def sibling_copy(s, origin_z, src=None, arriving=False):
        core = 1 - at.core if arriving else at.core
        block = c_all.at[at.feat(xh_of(s), origin_z, core)]
        k = s * nz + origin_z
        return remote(block if src is None else src, block, cs.at[k], cr.at[k], sibling)

    def y_copy(s, d, t, origin_y):
        block = x_all.at[at.node(origin_y, xl_of(s))]
        src = x_ref if (s == 0 and t == 1) else block
        return remote(src, block, ys.at[s, d, t - 1], yr.at[s, d, t - 1], along_y[d])

    z_sent, y_sent = [], []

    def z_start(s, d, t):
        copy = z_copy(s, d, t, origin(at.z, nz, d, t - 1))
        copy.start()
        z_sent.append(copy)

    def y_start(s, d, t):
        copy = y_copy(s, d, t, origin(at.y, ny, d, t - 1))
        copy.start()
        y_sent.append(copy)

    def across_copy(xh):
        return remote(c_ref, c_all.at[at.feat(xh, at.z, at.core)], xs, xr, across)

    def beside_copy(xl):
        return remote(x_ref, x_all.at[at.node(at.y, xl)], ls, lr, beside)

    across_copy(at.xh).start()
    beside_copy(at.xl).start()
    for d in (0, 1):
        z_start(0, d, 1)
        y_start(0, d, 1)
    sent_over = [sibling_copy(0, at.z, c_ref)]
    sent_over[0].start()
    c_all[at.j] = c_ref[...]
    x_all[at.i] = x_ref[...]
    beside_copy(1 - at.xl).wait_recv()
    for d in (0, 1):
        y_start(1, d, 1)
    across_copy(1 - at.xh).wait_recv()
    for d in (0, 1):
        z_start(1, d, 1)
    copy = sibling_copy(1, at.z)
    copy.start()
    sent_over.append(copy)

    for t in range(1, half_z + 1):
        for s in (0, 1):
            for d in (0, 1):
                if t <= last_y(s, d):
                    y_copy(s, d, t, origin(at.y, ny, d, t)).wait_recv()
                    if t < last_y(s, d):
                        y_start(s, d, t + 1)
                if t <= last_z(s, d):
                    origin_z = origin(at.z, nz, d, t)
                    z_copy(s, d, t, origin_z).wait_recv()
                    if t < last_z(s, d):
                        z_start(s, d, t + 1)
                    copy = sibling_copy(s, origin_z)
                    copy.start()
                    sent_over.append(copy)
    for s in (0, 1):
        for z in range(nz):
            sibling_copy(s, z, arriving=True).wait_recv()
    for copy in sent_over + z_sent + y_sent:
        copy.wait_send()
    across_copy(at.xh).wait_send()
    beside_copy(at.xl).wait_send()


def gather(n_nodes, n_feat, features, cotangent):
    rows, width = features.shape
    ny, nz = n_nodes // PAIR, n_feat // (PAIR * PAIR)
    dma = pltpu.SemaphoreType.DMA
    return pl.pallas_call(
        functools.partial(gather_kernel, n_nodes, n_feat),
        out_shape=(
            jax.ShapeDtypeStruct((n_nodes, rows, width), features.dtype),
            jax.ShapeDtypeStruct((n_feat, rows, width), cotangent.dtype),
        ),
        in_specs=[VMEM, VMEM],
        out_specs=(VMEM, VMEM),
        scratch_shapes=[
            dma,
            dma,
            dma((2, 2, nz // 2)),
            dma((2, 2, nz // 2)),
            dma((2 * nz,)),
            dma((2 * nz,)),
            dma,
            dma,
            dma((2, 2, ny // 2)),
            dma((2, 2, ny // 2)),
        ],
        compiler_params=pltpu.CompilerParams(collective_id=0, has_side_effects=True, vmem_limit_bytes=LIMIT),
        name="gather_blocks",
    )(features, cotangent)


def sparse_kernel(group, rows, cols, live, tiles, x_all, c_all, p_out, b_out, w_out, p_sum, b_sum):
    n_feat = p_out.shape[0]
    n_nodes = x_all.shape[0]

    def clear_p(r, carry):
        p_sum[r] = jnp.zeros(p_sum.shape[1:], jnp.float32)
        return carry

    def clear_b(c, carry):
        b_sum[c] = jnp.zeros(b_sum.shape[1:], jnp.float32)
        return carry

    lax.fori_loop(0, n_feat, clear_p, 0)
    lax.fori_loop(0, n_nodes, clear_b, 0)
    used = live[0]

    def step(g, carry):
        terms = []
        for u in range(group):
            k = g * group + u
            r, c = rows[k], cols[k]
            tile = tiles[k]
            ahead = jnp.dot(tile, x_all[c], preferred_element_type=jnp.float32)
            back = lax.dot_general(tile, c_all[r], (((0,), (0,)), ((), ())), preferred_element_type=jnp.float32)
            keep = k < used
            terms.append((r, c, jnp.where(keep, ahead, 0.0), jnp.where(keep, back, 0.0)))
        for r, c, ahead, back in terms:
            place = lax.rem(r, PAIR) * (n_feat // PAIR) + lax.div(r, PAIR)
            p_sum[place] += ahead
            b_sum[c] += back
        return carry

    lax.fori_loop(0, lax.div(used + group - 1, group), step, 0)

    def round_p(r, carry):
        p_out[r] = p_sum[r].astype(jnp.bfloat16)
        return carry

    lax.fori_loop(0, n_feat, round_p, 0)
    total = None
    for c in range(n_nodes):
        b = b_sum[c].astype(jnp.bfloat16)
        b_out[c] = b
        term = lax.dot_general(x_all[c], b, (((0,), (0,)), ((), ())), preferred_element_type=jnp.float32)
        total = term if total is None else total + term
    w_out[...] = total.reshape(w_out.shape)


def sparse(tile_rows, tile_cols, live, tiles, x_all, c_all):
    n_nodes, rows, width = x_all.shape
    n_feat = c_all.shape[0]
    return pl.pallas_call(
        functools.partial(sparse_kernel, 4),
        out_shape=(
            jax.ShapeDtypeStruct((n_feat, rows, width), jnp.bfloat16),
            jax.ShapeDtypeStruct((n_nodes, rows, width), jnp.bfloat16),
            jax.ShapeDtypeStruct((n_nodes, width // n_nodes, width), jnp.float32),
        ),
        in_specs=[SMEM, SMEM, SMEM, VMEM, VMEM, VMEM],
        out_specs=(VMEM, VMEM, VMEM),
        scratch_shapes=[
            pltpu.VMEM((n_feat, rows, width), jnp.float32),
            pltpu.VMEM((n_nodes, rows, width), jnp.float32),
        ],
        compiler_params=pltpu.CompilerParams(vmem_limit_bytes=LIMIT),
        name="sparse_products",
    )(tile_rows, tile_cols, live, tiles, x_all, c_all)


def split_dot(value, weight, dims):
    high = value.astype(jnp.bfloat16)
    low = (value - high.astype(jnp.float32)).astype(jnp.bfloat16)
    return sum(
        lax.dot_general(part, weight, (dims, ((), ())), preferred_element_type=jnp.float32) for part in (high, low)
    )


def wide(value):
    return value.astype(jnp.float32)


def sum_kernel(
    n_nodes, n_feat, scale,
    p_ref, b_ref, w_ref, weight_ref, out_ref, fg_ref, wg_ref,
    c_rx, x_tx, x_rx, z_tx, z_rx, y_rx, l_tx, l_rx, w1, w4, wz, wn,
    cs, cr, xs, xr, zs, zr, ys, yr, ls, lr, w1s, w1r, w4s, w4r, wzs, wzr, wns, wnr,
):
    at = Place(n_nodes, n_feat)
    nz, ny = at.nz, at.ny
    sibling = (at.i, at.feat(at.xh, at.z, 1 - at.core))
    across = (at.i, at.feat(1 - at.xh, at.z, at.core))
    slanted = (at.i, at.feat(1 - at.xh, at.z, 1 - at.core))
    beside = (at.node(at.y, 1 - at.xl), at.j)

    def node_peer(t):
        i = lax.rem(at.i + t, n_nodes)
        return i, (i, at.j)

    def y_peer(t):
        y = lax.rem(at.y + t, ny)
        return y, (at.node(y, at.xl), at.j)

    def z_peer(t):
        k = lax.div(nz - 1 - t, 2) + lax.rem(nz - 1 - t, 2)
        off = lax.rem(t, 2) * (nz - 2 * k) + k
        z = lax.rem(at.z + off, nz)
        return z, (at.i, at.feat(at.xh, z, at.core))

    greet(
        [sibling, across, slanted]
        + [node_peer(t)[1] for t in range(1, n_nodes)]
        + [z_peer(t)[1] for t in range(nz - 1)]
    )

    def loop(start, stop, body):
        lax.fori_loop(start, stop, lambda t, carry: (body(t), carry)[1], 0)

    def w1_copy(t):
        i, device = node_peer(t)
        return remote(w_ref.at[i], w1.at[at.i], w1s.at[i], w1r.at[at.i], device)

    loop(1, n_nodes, lambda t: w1_copy(t).start())

    def c_copy(xh, z):
        slot = xh * nz + z
        return remote(
            p_ref.at[(1 - at.core) * 2 * nz + slot], c_rx.at[slot], cs.at[slot], cr.at[slot], sibling
        )

    def own_p(xh, z):
        return wide(p_ref[(at.core * 2 + xh) * nz + z])

    loop(0, nz - 1, lambda t: c_copy(1 - at.xh, z_peer(t)[0]).start())
    c_copy(1 - at.xh, at.z).start()
    loop(0, nz - 1, lambda t: c_copy(at.xh, z_peer(t)[0]).start())
    c_copy(at.xh, at.z).start()

    def y_copy(t):
        y, device = y_peer(t)
        return remote(b_ref.at[pl.ds(y * PAIR, PAIR)], y_rx.at[at.y], ys.at[y], yr.at[at.y], device)

    loop(1, ny, lambda t: y_copy(t).start())

    def x_copy(z):
        return remote(x_tx.at[z], x_rx.at[z], xs.at[z], xr.at[z], across)

    def x_step(z):
        c_copy(1 - at.xh, z).wait_recv()
        x_tx[z] = (own_p(1 - at.xh, z) + wide(c_rx[(1 - at.xh) * nz + z])).astype(jnp.bfloat16)
        x_copy(z).start()

    loop(0, nz - 1, lambda t: x_step(z_peer(t)[0]))
    x_step(at.z)

    def w1_arrival(t):
        i, device = node_peer(t)
        remote(w_ref.at[at.i], w1.at[i], w1s.at[i], w1r.at[i], device).wait_recv()

    w1[at.i] = w_ref[at.i]
    loop(1, n_nodes, w1_arrival)
    me4 = at.xh * 2 + at.core
    w4[me4] = jnp.sum(w1[...], axis=0)
    four = [
        (at.xh * 2 + 1 - at.core, sibling),
        ((1 - at.xh) * 2 + at.core, across),
        ((1 - at.xh) * 2 + 1 - at.core, slanted),
    ]
    for slot, device in four:
        remote(w4.at[me4], w4.at[me4], w4s.at[slot], w4r.at[me4], device).start()

    def z_copy(t):
        z, device = z_peer(t)
        return remote(z_tx.at[z], z_rx.at[at.z], zs.at[z], zr.at[at.z], device)

    def four_sum(z):
        c_copy(at.xh, z).wait_recv()
        x_copy(z).wait_recv()
        return own_p(at.xh, z) + wide(c_rx[at.xh * nz + z]) + wide(x_rx[z])

    def z_step(t):
        z = z_peer(t)[0]
        z_tx[z] = four_sum(z).astype(jnp.bfloat16)
        z_copy(t).start()

    loop(0, nz - 1, z_step)
    mine = four_sum(at.z)

    for slot, device in four:
        remote(w4.at[slot], w4.at[slot], w4s.at[slot], w4r.at[slot], device).wait_recv()
    wz[at.z] = jnp.sum(w4[...], axis=0)

    def wz_copy(t):
        z, device = z_peer(t)
        return remote(wz.at[at.z], wz.at[at.z], wzs.at[z], wzr.at[at.z], device)

    loop(0, nz - 1, lambda t: wz_copy(t).start())

    def y_arrival(t):
        y, device = y_peer(t)
        remote(b_ref.at[pl.ds(y * PAIR, PAIR)], y_rx.at[y], ys.at[y], yr.at[y], device).wait_recv()

    loop(1, ny, y_arrival)

    def y_sum(xl):
        def add(t, total):
            return total + wide(y_rx[y_peer(t)[0], xl])

        return lax.fori_loop(1, ny, add, wide(b_ref[at.node(at.y, xl)]))

    l_copy = remote(l_tx, l_rx, ls, lr, beside)
    l_tx[...] = y_sum(1 - at.xl).astype(jnp.bfloat16)
    l_copy.start()
    near = y_sum(at.xl)

    def wz_arrival(t):
        z, device = z_peer(t)
        remote(wz.at[z], wz.at[z], wzs.at[z], wzr.at[z], device).wait_recv()

    loop(0, nz - 1, wz_arrival)
    wn[at.i] = jnp.sum(wz[...], axis=0) * scale

    def wn_copy(t):
        i, device = node_peer(t)
        return remote(wn.at[at.i], wn.at[at.i], wns.at[i], wnr.at[at.i], device)

    loop(1, n_nodes, lambda t: wn_copy(t).start())

    l_copy.wait_recv()
    fg_ref[...] = split_dot(near + wide(l_rx[...]), weight_ref[...], ((1,), (1,))).astype(fg_ref.dtype)

    def z_arrival(t, total):
        z, device = z_peer(t)
        remote(z_tx.at[z], z_rx.at[z], zs.at[z], zr.at[z], device).wait_recv()
        return total + wide(z_rx[z])

    whole = lax.fori_loop(0, nz - 1, z_arrival, mine)
    out_ref[...] = split_dot(whole, weight_ref[...], ((1,), (0,))).astype(out_ref.dtype)

    def wn_arrival(t):
        i, device = node_peer(t)
        remote(wn.at[i], wn.at[i], wns.at[i], wnr.at[i], device).wait_recv()

    loop(1, n_nodes, wn_arrival)
    wg_ref[...] = wn[...]

    loop(1, n_nodes, lambda t: w1_copy(t).wait_send())
    for xh in (0, 1):
        loop(0, nz, lambda z: c_copy(xh, z).wait_send())
    loop(1, ny, lambda t: y_copy(t).wait_send())
    loop(0, nz, lambda z: x_copy(z).wait_send())
    for slot, device in four:
        remote(w4.at[me4], w4.at[me4], w4s.at[slot], w4r.at[me4], device).wait_send()
    loop(0, nz - 1, lambda t: z_copy(t).wait_send())
    loop(0, nz - 1, lambda t: wz_copy(t).wait_send())
    l_copy.wait_send()
    loop(1, n_nodes, lambda t: wn_copy(t).wait_send())


def sum_up(n_nodes, n_feat, scale, partial, back, term, weight):
    rows, width = partial.shape[1:]
    ny, nz = n_nodes // PAIR, n_feat // (PAIR * PAIR)
    dma = pltpu.SemaphoreType.DMA
    share = width // n_nodes

    def blocks(*lead):
        return pltpu.VMEM((*lead, rows, width), jnp.bfloat16)

    def shares(count):
        return pltpu.VMEM((count, share, width), jnp.float32)

    counts = (2 * nz, nz, nz, ny, None, n_nodes, 4, nz, n_nodes)
    sems = []
    for count in counts:
        sems += [dma if count is None else dma((count,))] * 2
    return pl.pallas_call(
        functools.partial(sum_kernel, n_nodes, n_feat, scale),
        out_shape=(
            jax.ShapeDtypeStruct((rows, width), jnp.bfloat16),
            jax.ShapeDtypeStruct((rows, width), jnp.bfloat16),
            jax.ShapeDtypeStruct((n_nodes, share, width), jnp.float32),
        ),
        in_specs=[VMEM] * 4,
        out_specs=(VMEM,) * 3,
        scratch_shapes=[
            blocks(2 * nz),
            blocks(nz),
            blocks(nz),
            blocks(nz),
            blocks(nz),
            blocks(ny, PAIR),
            blocks(),
            blocks(),
            shares(n_nodes),
            shares(4),
            shares(nz),
            shares(n_nodes),
        ]
        + sems,
        compiler_params=pltpu.CompilerParams(collective_id=1, has_side_effects=True, vmem_limit_bytes=LIMIT),
        name="sum_blocks",
    )(partial, back, term, weight)


def body(n_nodes, n_feat, features, weight, tiles, tile_rows, tile_cols, live, cotangent):
    scale = 1.0 / math.sqrt(features.shape[0] * n_nodes * n_feat)
    x_all, c_all = gather(n_nodes, n_feat, features, cotangent)
    partial, back, term = sparse(tile_rows, tile_cols, live, tiles, x_all, c_all)
    output, feature_grad, weight_grad = sum_up(n_nodes, n_feat, scale, partial, back, term, weight)
    return output, feature_grad, weight_grad.reshape(weight.shape)


def solution(mesh):
    in_specs = (
        P(("feat", "nodes"), None),
        P(),
        P(("nodes", "feat"), None, None),
        P(("nodes", "feat")),
        P(("nodes", "feat")),
        P(("nodes", "feat")),
        P(("nodes", "feat"), None),
    )
    out_specs = (P(("nodes", "feat"), None), P(("feat", "nodes"), None), P())
    step = functools.partial(body, mesh.shape["nodes"], mesh.shape["feat"])
    return jax.shard_map(step, mesh=mesh, in_specs=in_specs, out_specs=out_specs, check_vma=False)
```

```python
import functools
import math

import jax
import jax.numpy as jnp
from jax import lax
from jax.experimental import pallas as pl
from jax.experimental.pallas import tpu as pltpu
from jax.sharding import PartitionSpec as P

MESH = pl.DeviceIdType.MESH
VMEM = pl.BlockSpec(memory_space=pltpu.VMEM)
ANY = pl.BlockSpec(memory_space=pl.ANY)
SMEM = pl.BlockSpec(memory_space=pltpu.SMEM)
LIMIT = 52 * 1024 * 1024
GROUP = 4
PAIR = 2


class Place:
    def __init__(self, n_nodes, n_feat):
        self.n_nodes, self.n_feat = n_nodes, n_feat
        self.ny, self.nz = n_nodes // PAIR, n_feat // (PAIR * PAIR)
        self.i, self.j = lax.axis_index("nodes"), lax.axis_index("feat")
        self.y, self.xl = lax.div(self.i, PAIR), lax.rem(self.i, PAIR)
        self.xh = lax.div(self.j, PAIR * self.nz)
        self.z = lax.rem(lax.div(self.j, PAIR), self.nz)
        self.core = lax.rem(self.j, PAIR)

    def node(self, y, xl):
        return y * PAIR + xl

    def feat(self, xh, z, core):
        return (xh * self.nz + z) * PAIR + core


def greet(partners):
    barrier = pltpu.get_barrier_semaphore()
    for device in partners:
        pl.semaphore_signal(barrier, inc=1, device_id=device, device_id_type=MESH)
    pl.semaphore_wait(barrier, len(partners))


def remote(src, dst, send_sem, recv_sem, device):
    return pltpu.make_async_remote_copy(
        src_ref=src, dst_ref=dst, send_sem=send_sem, recv_sem=recv_sem, device_id=device, device_id_type=MESH
    )


def wide(value):
    return value.astype(jnp.float32)


def split_dot(value, weight, dims):
    high = value.astype(jnp.bfloat16)
    low = (value - wide(high)).astype(jnp.bfloat16)
    return sum(
        lax.dot_general(part, weight, (dims, ((), ())), preferred_element_type=jnp.float32) for part in (high, low)
    )


def chains(tile_rows, tile_cols, live, row_count, col_count):
    slot = jnp.arange(tile_rows.shape[0], dtype=jnp.int32)

    def before(values):
        same = (values[:, None] == values[None, :]) & (slot[None, :] < slot[:, None])
        return jnp.max(jnp.where(same, slot[None, :], -1), axis=1)

    def last(values, count):
        places = jnp.arange(count, dtype=jnp.int32)
        same = (values[None, :] == places[:, None]) & (slot[None, :] < live[0])
        return jnp.max(jnp.where(same, slot[None, :], -1), axis=1)

    return jnp.concatenate(
        [
            tile_rows,
            tile_cols,
            before(tile_rows),
            before(tile_cols),
            last(tile_rows, row_count),
            last(tile_cols, col_count),
        ]
    )


def kernel(
    n_nodes, n_feat, scale,
    index, x_ref, c_ref, weight_ref, tiles_ref, out_ref, fg_ref, wg_ref,
    tiles, x_all, c_all, ahead, back, p_tx, b_tx, c_rx, x_tx, x_rx, z_tx, z_rx, y_rx, l_tx, l_rx,
    w0, w1, w4_tx, w4, wz, w5, wn, tile_sem,
    gxs, gxr, gzs, gzr, gcs, gcr, gls, glr, gys, gyr,
    cs, cr, xs, xr, zs, zr, ys, yr, ls, lr, w1s, w1r, w4s, w4r, wzs, wzr, w5s, w5r, wns, wnr,
):
    at = Place(n_nodes, n_feat)
    nz, ny = at.nz, at.ny
    slots = tiles.shape[0]
    before_row, before_col, last_row, last_col = 2 * slots, 3 * slots, 4 * slots, 4 * slots + n_feat
    z_near = [lax.rem(at.z + 1, nz), lax.rem(at.z + nz - 1, nz)]
    y_near = [lax.rem(at.y + 1, ny), lax.rem(at.y + ny - 1, ny)]
    sibling = (at.i, at.feat(at.xh, at.z, 1 - at.core))
    across = (at.i, at.feat(1 - at.xh, at.z, at.core))
    slanted = (at.i, at.feat(1 - at.xh, at.z, 1 - at.core))
    beside = (at.node(at.y, 1 - at.xl), at.j)
    along_z = [(at.i, at.feat(at.xh, z, at.core)) for z in z_near]
    along_y = [(at.node(y, at.xl), at.j) for y in y_near]

    def node_peer(t):
        i = lax.rem(at.i + t, n_nodes)
        return i, (i, at.j)

    def y_peer(t):
        y = lax.rem(at.y + t, ny)
        return y, (at.node(y, at.xl), at.j)

    def z_peer(t):
        k = lax.div(nz - 1 - t, 2) + lax.rem(nz - 1 - t, 2)
        off = lax.rem(t, 2) * (nz - 2 * k) + k
        z = lax.rem(at.z + off, nz)
        return z, (at.i, at.feat(at.xh, z, at.core))

    def loop(start, stop, body):
        lax.fori_loop(start, stop, lambda t, carry: (body(t), carry)[1], 0)

    tile_copy = pltpu.make_async_copy(tiles_ref, tiles, tile_sem)
    tile_copy.start()
    greet(
        [sibling, across, slanted]
        + [node_peer(t)[1] for t in range(1, n_nodes)]
        + [z_peer(t)[1] for t in range(nz - 1)]
    )

    half_z, half_y = nz // 2, ny // 2

    def last_z(s, d):
        return half_z if s == d else nz - 1 - half_z

    def last_y(s, d):
        return half_y if s == d else ny - 1 - half_y

    def origin(place, count, d, t):
        return lax.rem(place + (count - t if d == 0 else t), count)

    def xh_of(s):
        return at.xh if s == 0 else 1 - at.xh

    def xl_of(s):
        return at.xl if s == 0 else 1 - at.xl

    def gz_copy(s, d, t, origin_z):
        block = c_all.at[at.feat(xh_of(s), origin_z, at.core)]
        src = c_ref if (s == 0 and t == 1) else block
        return remote(src, block, gzs.at[s, d, t - 1], gzr.at[s, d, t - 1], along_z[d])

    def sibling_copy(s, origin_z, src=None, arriving=False):
        core = 1 - at.core if arriving else at.core
        block = c_all.at[at.feat(xh_of(s), origin_z, core)]
        k = s * nz + origin_z
        return remote(block if src is None else src, block, gcs.at[k], gcr.at[k], sibling)

    def gy_copy(s, d, t, origin_y):
        block = x_all.at[at.node(origin_y, xl_of(s))]
        src = x_ref if (s == 0 and t == 1) else block
        return remote(src, block, gys.at[s, d, t - 1], gyr.at[s, d, t - 1], along_y[d])

    z_sent, y_sent = [], []

    def z_start(s, d, t):
        copy = gz_copy(s, d, t, origin(at.z, nz, d, t - 1))
        copy.start()
        z_sent.append(copy)

    def y_start(s, d, t):
        copy = gy_copy(s, d, t, origin(at.y, ny, d, t - 1))
        copy.start()
        y_sent.append(copy)

    def across_copy(xh):
        return remote(c_ref, c_all.at[at.feat(xh, at.z, at.core)], gxs, gxr, across)

    def beside_copy(xl):
        return remote(x_ref, x_all.at[at.node(at.y, xl)], gls, glr, beside)

    across_copy(at.xh).start()
    beside_copy(at.xl).start()
    for d in (0, 1):
        z_start(0, d, 1)
        y_start(0, d, 1)
    sent_over = [sibling_copy(0, at.z, c_ref)]
    sent_over[0].start()
    c_all[at.j] = c_ref[...]
    x_all[at.i] = x_ref[...]
    beside_copy(1 - at.xl).wait_recv()
    for d in (0, 1):
        y_start(1, d, 1)
    across_copy(1 - at.xh).wait_recv()
    for d in (0, 1):
        z_start(1, d, 1)
    copy = sibling_copy(1, at.z)
    copy.start()
    sent_over.append(copy)


    def y_arrive(t):
        for s in (0, 1):
            for d in (0, 1):
                if t <= last_y(s, d):
                    gy_copy(s, d, t, origin(at.y, ny, d, t)).wait_recv()
                    if t < last_y(s, d):
                        y_start(s, d, t + 1)

    def z_arrive(s, d, t):
        if t <= last_z(s, d):
            origin_z = origin(at.z, nz, d, t)
            gz_copy(s, d, t, origin_z).wait_recv()
            if t < last_z(s, d):
                z_start(s, d, t + 1)
            over = sibling_copy(s, origin_z)
            over.start()
            sent_over.append(over)

    ways = [(s, d) for s in (0, 1) for d in (0, 1)]
    split = max(1, half_z - 2)
    for t in range(1, max(split, half_y) + 1):
        if t <= half_y:
            y_arrive(t)
        if t <= split:
            for s, d in ways:
                z_arrive(s, d, t)

    def add_chain(sums, terms, before, k0):
        for u, term in enumerate(terms):
            prev = index[before + k0 + u]
            sums[k0 + u] = term + jnp.where(prev >= 0, sums[jnp.maximum(prev, 0)], 0.0)

    def ahead_step(g):
        terms = [
            jnp.dot(tiles[g * GROUP + u], x_all[index[slots + g * GROUP + u]], preferred_element_type=jnp.float32)
            for u in range(GROUP)
        ]
        add_chain(ahead, terms, before_row, g * GROUP)

    def back_step(g):
        terms = [
            lax.dot_general(
                tiles[g * GROUP + u], c_all[index[g * GROUP + u]], (((0,), (0,)), ((), ())),
                preferred_element_type=jnp.float32,
            )
            for u in range(GROUP)
        ]
        add_chain(back, terms, before_col, g * GROUP)

    def own_p(xh, z, core):
        k = index[last_row + at.feat(xh, z, core)]
        return jnp.where(k >= 0, ahead[jnp.maximum(k, 0)], 0.0)

    def own_b(y, xl):
        k = index[last_col + at.node(y, xl)]
        return jnp.where(k >= 0, back[jnp.maximum(k, 0)], 0.0)

    groups = slots // GROUP
    tile_copy.wait()
    done = 0
    rest = [(s, d, t) for t in range(split + 1, half_z) for s, d in ways]
    for n, (s, d, t) in enumerate(rest):
        z_arrive(s, d, t)
        upto = groups * (n + 1) // len(rest)
        loop(done, upto, ahead_step)
        done = upto
    loop(done, groups, ahead_step)

    def c_copy(xh, z):
        slot = xh * nz + z
        return remote(p_tx.at[slot], c_rx.at[slot], cs.at[slot], cr.at[slot], sibling)

    def c_step(xh, z):
        p_tx[xh * nz + z] = own_p(xh, z, 1 - at.core).astype(jnp.bfloat16)
        c_copy(xh, z).start()

    loop(0, nz - 1, lambda t: c_step(1 - at.xh, z_peer(t)[0]))
    c_step(1 - at.xh, at.z)
    for s, d in ways:
        z_arrive(s, d, half_z)
    loop(0, nz - 1, lambda t: c_step(at.xh, z_peer(t)[0]))
    c_step(at.xh, at.z)

    def x_copy(z):
        return remote(x_tx.at[z], x_rx.at[z], xs.at[z], xr.at[z], across)

    def x_step(z):
        c_copy(1 - at.xh, z).wait_recv()
        x_tx[z] = (own_p(1 - at.xh, z, at.core) + wide(c_rx[(1 - at.xh) * nz + z])).astype(jnp.bfloat16)
        x_copy(z).start()

    loop(0, nz - 1, lambda t: x_step(z_peer(t)[0]))
    x_step(at.z)

    for s in (0, 1):
        for z in range(nz):
            sibling_copy(s, z, arriving=True).wait_recv()
    loop(0, groups, back_step)
    total = None
    for i in range(n_nodes):
        b_tx[i] = own_b(i // PAIR, i % PAIR).astype(jnp.bfloat16)
        term = lax.dot_general(x_all[i], b_tx[i], (((0,), (0,)), ((), ())), preferred_element_type=jnp.float32)
        total = term if total is None else total + term
    w0[...] = total.astype(w0.dtype).reshape(w0.shape)

    def w1_copy(t):
        i, device = node_peer(t)
        return remote(w0.at[i], w1.at[at.i], w1s.at[i], w1r.at[at.i], device)

    loop(1, n_nodes, lambda t: w1_copy(t).start())

    def y_copy(t):
        y, device = y_peer(t)
        return remote(b_tx.at[pl.ds(y * PAIR, PAIR)], y_rx.at[at.y], ys.at[y], yr.at[at.y], device)

    loop(1, ny, lambda t: y_copy(t).start())

    def z_copy(t):
        z, device = z_peer(t)
        return remote(z_tx.at[z], z_rx.at[at.z], zs.at[z], zr.at[at.z], device)

    def four_sum(z):
        c_copy(at.xh, z).wait_recv()
        x_copy(z).wait_recv()
        return own_p(at.xh, z, at.core) + wide(c_rx[at.xh * nz + z]) + wide(x_rx[z])

    def z_step(t):
        z = z_peer(t)[0]
        z_tx[z] = four_sum(z).astype(jnp.bfloat16)
        z_copy(t).start()

    first, second = nz // 3, 2 * nz // 3
    loop(0, first, z_step)

    def w1_arrival(t):
        i, device = node_peer(t)
        remote(w0.at[i], w1.at[i], w1s.at[i], w1r.at[i], device).wait_recv()

    w1[at.i] = w0[at.i]
    loop(1, n_nodes, w1_arrival)
    me4 = at.xh * 2 + at.core
    shared = jnp.sum(wide(w1[...]), axis=0)
    for slot in range(4):
        row, column = slot // 2 * 8, slot % 2 * 128
        w4_tx[slot] = shared[row : row + 8, column : column + 128]
    w4[me4] = w4_tx[me4]
    four = [
        (at.xh * 2 + 1 - at.core, sibling),
        ((1 - at.xh) * 2 + at.core, across),
        ((1 - at.xh) * 2 + 1 - at.core, slanted),
    ]

    def w4_copy(slot, device):
        return remote(w4_tx.at[slot], w4.at[me4], w4s.at[slot], w4r.at[me4], device)

    for slot, device in four:
        w4_copy(slot, device).start()
    loop(first, second, z_step)

    for slot, device in four:
        remote(w4_tx.at[slot], w4.at[slot], w4s.at[slot], w4r.at[slot], device).wait_recv()
    wz[at.z] = jnp.sum(w4[...], axis=0)

    def wz_copy(t):
        z, device = z_peer(t)
        return remote(wz.at[at.z], wz.at[at.z], wzs.at[z], wzr.at[at.z], device)

    loop(0, nz - 1, lambda t: wz_copy(t).start())
    loop(second, nz - 1, z_step)
    mine = four_sum(at.z)

    def wz_arrival(t):
        z, device = z_peer(t)
        remote(wz.at[z], wz.at[z], wzs.at[z], wzr.at[z], device).wait_recv()

    loop(0, nz - 1, wz_arrival)
    w5[me4] = jnp.sum(wz[...], axis=0) * scale

    def w5_copy(slot, device):
        return remote(w5.at[me4], w5.at[me4], w5s.at[slot], w5r.at[me4], device)

    for slot, device in four:
        w5_copy(slot, device).start()
    for slot, device in four:
        remote(w5.at[slot], w5.at[slot], w5s.at[slot], w5r.at[slot], device).wait_recv()
    wn[at.i] = jnp.concatenate(
        [jnp.concatenate([w5[2 * half], w5[2 * half + 1]], axis=1) for half in (0, 1)], axis=0
    ).astype(wn.dtype)

    def wn_copy(t):
        i, device = node_peer(t)
        return remote(wn.at[at.i], wn.at[at.i], wns.at[i], wnr.at[at.i], device)

    loop(1, n_nodes, lambda t: wn_copy(t).start())

    def y_arrival(t):
        y, device = y_peer(t)
        remote(b_tx.at[pl.ds(y * PAIR, PAIR)], y_rx.at[y], ys.at[y], yr.at[y], device).wait_recv()

    loop(1, ny, y_arrival)

    def y_sum(xl):
        def add(t, total):
            return total + wide(y_rx[y_peer(t)[0], xl])

        return lax.fori_loop(1, ny, add, own_b(at.y, xl))

    l_copy = remote(l_tx, l_rx, ls, lr, beside)
    l_tx[...] = y_sum(1 - at.xl).astype(jnp.bfloat16)
    l_copy.start()
    near = y_sum(at.xl)

    def z_arrival(t, total):
        z, device = z_peer(t)
        remote(z_tx.at[z], z_rx.at[z], zs.at[z], zr.at[z], device).wait_recv()
        return total + wide(z_rx[z])

    whole = lax.fori_loop(0, nz - 1, z_arrival, mine)
    out_ref[...] = split_dot(whole, weight_ref[...], ((1,), (0,))).astype(out_ref.dtype)

    l_copy.wait_recv()
    fg_ref[...] = split_dot(near + wide(l_rx[...]), weight_ref[...], ((1,), (1,))).astype(fg_ref.dtype)

    def wn_arrival(t):
        i, device = node_peer(t)
        remote(wn.at[i], wn.at[i], wns.at[i], wnr.at[i], device).wait_recv()

    loop(1, n_nodes, wn_arrival)
    wg_ref[...] = wide(wn[...])

    for sent in sent_over + z_sent + y_sent:
        sent.wait_send()
    across_copy(at.xh).wait_send()
    beside_copy(at.xl).wait_send()
    for xh in (0, 1):
        loop(0, nz, lambda z: c_copy(xh, z).wait_send())
    loop(0, nz, lambda z: x_copy(z).wait_send())
    loop(1, n_nodes, lambda t: w1_copy(t).wait_send())
    loop(1, ny, lambda t: y_copy(t).wait_send())
    loop(0, nz - 1, lambda t: z_copy(t).wait_send())
    for slot, device in four:
        w4_copy(slot, device).wait_send()
        w5_copy(slot, device).wait_send()
    loop(0, nz - 1, lambda t: wz_copy(t).wait_send())
    l_copy.wait_send()
    loop(1, n_nodes, lambda t: wn_copy(t).wait_send())


def body(n_nodes, n_feat, features, weight, tiles, tile_rows, tile_cols, live, cotangent):
    rows, width = features.shape
    scale = 1.0 / math.sqrt(rows * n_nodes * n_feat)
    ny, nz = n_nodes // PAIR, n_feat // (PAIR * PAIR)
    slots, side = tiles.shape[:2]
    share = width // n_nodes
    dma = pltpu.SemaphoreType.DMA

    def blocks(*lead, kind=jnp.bfloat16):
        return pltpu.VMEM((*lead, rows, width), kind)

    def shares(count, kind):
        return pltpu.VMEM((count, share, width), kind)

    def pieces(count):
        return pltpu.VMEM((count, share // 2, width // 2), jnp.float32)

    def pairs(*counts):
        return [sem for count in counts for sem in [dma(count) if count else dma] * 2]

    index = chains(tile_rows, tile_cols, live, n_feat, n_nodes)
    output, feature_grad, weight_grad = pl.pallas_call(
        functools.partial(kernel, n_nodes, n_feat, scale),
        out_shape=(
            jax.ShapeDtypeStruct((rows, width), jnp.bfloat16),
            jax.ShapeDtypeStruct((rows, width), jnp.bfloat16),
            jax.ShapeDtypeStruct((n_nodes, share, width), jnp.float32),
        ),
        in_specs=[SMEM, VMEM, VMEM, VMEM, ANY],
        out_specs=(VMEM,) * 3,
        scratch_shapes=[
            pltpu.VMEM(tiles.shape, tiles.dtype),
            blocks(n_nodes),
            blocks(n_feat),
            blocks(slots, kind=jnp.float32),
            blocks(slots, kind=jnp.float32),
            blocks(2 * nz),
            blocks(n_nodes),
            blocks(2 * nz),
            blocks(nz),
            blocks(nz),
            blocks(nz),
            blocks(nz),
            blocks(ny, PAIR),
            blocks(),
            blocks(),
            shares(n_nodes, jnp.bfloat16),
            shares(n_nodes, jnp.bfloat16),
            pieces(4),
            pieces(4),
            pieces(nz),
            pieces(4),
            shares(n_nodes, jnp.bfloat16),
            dma,
        ]
        + pairs(None, (2, 2, nz // 2), (2 * nz,), None, (2, 2, ny // 2))
        + pairs((2 * nz,), (nz,), (nz,), (ny,), None)
        + pairs((n_nodes,), (4,), (nz,), (4,), (n_nodes,)),
        compiler_params=pltpu.CompilerParams(collective_id=0, has_side_effects=True, vmem_limit_bytes=LIMIT),
        name="graph_layer",
    )(index, features, cotangent, weight, tiles)
    return output, feature_grad, weight_grad.reshape(weight.shape)


def solution(mesh):
    in_specs = (
        P(("feat", "nodes"), None),
        P(),
        P(("nodes", "feat"), None, None),
        P(("nodes", "feat")),
        P(("nodes", "feat")),
        P(("nodes", "feat")),
        P(("nodes", "feat"), None),
    )
    out_specs = (P(("nodes", "feat"), None), P(("feat", "nodes"), None), P())
    step = functools.partial(body, mesh.shape["nodes"], mesh.shape["feat"])
    return jax.shard_map(step, mesh=mesh, in_specs=in_specs, out_specs=out_specs, check_vma=False)
```

```python
import functools
import math

import jax
import jax.numpy as jnp
from jax import lax
from jax.experimental import pallas as pl
from jax.experimental.pallas import tpu as pltpu
from jax.sharding import PartitionSpec as P

MESH = pl.DeviceIdType.MESH
VMEM = pl.BlockSpec(memory_space=pltpu.VMEM)
ANY = pl.BlockSpec(memory_space=pl.ANY)
LIMIT = 60 * 1024 * 1024
LANES = 128
GROUP = 4
PAIR = 2


class Place:
    def __init__(self, n_nodes, n_feat):
        self.n_nodes, self.n_feat = n_nodes, n_feat
        self.ny, self.nz = n_nodes // PAIR, n_feat // (PAIR * PAIR)
        self.i, self.j = lax.axis_index("nodes"), lax.axis_index("feat")
        self.y, self.xl = lax.div(self.i, PAIR), lax.rem(self.i, PAIR)
        self.xh = lax.div(self.j, PAIR * self.nz)
        self.z = lax.rem(lax.div(self.j, PAIR), self.nz)
        self.core = lax.rem(self.j, PAIR)

    def node(self, y, xl):
        return y * PAIR + xl

    def feat(self, xh, z, core):
        return (xh * self.nz + z) * PAIR + core


def greet(partners):
    barrier = pltpu.get_barrier_semaphore()
    for device in partners:
        pl.semaphore_signal(barrier, inc=1, device_id=device, device_id_type=MESH)
    pl.semaphore_wait(barrier, len(partners))


def remote(src, dst, send_sem, recv_sem, device):
    return pltpu.make_async_remote_copy(
        src_ref=src, dst_ref=dst, send_sem=send_sem, recv_sem=recv_sem, device_id=device, device_id_type=MESH
    )


def wide(value):
    return value.astype(jnp.float32)


def split_dot(value, weight, dims):
    high = value.astype(jnp.bfloat16)
    low = (value - wide(high)).astype(jnp.bfloat16)
    return sum(
        lax.dot_general(part, weight, (dims, ((), ())), preferred_element_type=jnp.float32) for part in (high, low)
    )


def spread_chains(rows, cols, live, row_count, col_count, row_mat, col_mat, chain):
    slots = rows.shape[0]

    def fill(k, carry):
        row_mat[pl.ds(k, 1), :] = jnp.full((1, LANES), rows[k], jnp.int32)
        col_mat[pl.ds(k, 1), :] = jnp.full((1, LANES), cols[k], jnp.int32)
        return carry

    row_mat[...] = jnp.full(row_mat.shape, -1, jnp.int32)
    col_mat[...] = jnp.full(col_mat.shape, -1, jnp.int32)
    lax.fori_loop(0, slots, fill, 0)
    line = lax.broadcasted_iota(jnp.int32, (LANES, LANES), 0)
    slot = lax.broadcasted_iota(jnp.int32, (LANES, LANES), 1)

    def best(keep):
        return jnp.max(jnp.where(keep, slot, -1), axis=1, keepdims=True)

    found = []
    for mat in (row_mat, col_mat):
        along, across = mat[...], mat[...].T
        found.append((best((along == across) & (slot < line)), best((across == line) & (slot < live))))
    (before_row, last_row), (before_col, last_col) = found
    chain[...] = jnp.where(
        slot == 0, before_row, jnp.where(slot == 1, before_col, jnp.where(slot == 2, last_row, last_col))
    )


def kernel(
    n_nodes, n_feat, scale,
    rows_ref, cols_ref, live_ref, x_ref, c_ref, weight_in, tiles_ref, out_ref, fg_ref, wg_ref,
    rows, cols, live, row_mat, col_mat, chain, index, weight_ref, tiles, x_all, c_all, ahead, back, p_tx, b_tx, c_rx, x_tx, x_rx, z_tx, z_rx, y_rx, l_tx, l_rx,
    w0, w1, w4_tx, w4, wz, w5, wn, load_sem, tile_sem,
    gxs, gxr, gzs, gzr, gcs, gcr, gls, glr, gys, gyr,
    cs, cr, xs, xr, zs, zr, ys, yr, ls, lr, w1s, w1r, w4s, w4r, wzs, wzr, w5s, w5r, wns, wnr,
):
    at = Place(n_nodes, n_feat)
    nz, ny = at.nz, at.ny
    slots = tiles.shape[0]
    z_near = [lax.rem(at.z + 1, nz), lax.rem(at.z + nz - 1, nz)]
    y_near = [lax.rem(at.y + 1, ny), lax.rem(at.y + ny - 1, ny)]
    sibling = (at.i, at.feat(at.xh, at.z, 1 - at.core))
    across = (at.i, at.feat(1 - at.xh, at.z, at.core))
    slanted = (at.i, at.feat(1 - at.xh, at.z, 1 - at.core))
    beside = (at.node(at.y, 1 - at.xl), at.j)
    along_z = [(at.i, at.feat(at.xh, z, at.core)) for z in z_near]
    along_y = [(at.node(y, at.xl), at.j) for y in y_near]

    def node_peer(t):
        i = lax.rem(at.i + t, n_nodes)
        return i, (i, at.j)

    def y_peer(t):
        y = lax.rem(at.y + t, ny)
        return y, (at.node(y, at.xl), at.j)

    def z_peer(t):
        k = lax.div(nz - 1 - t, 2) + lax.rem(nz - 1 - t, 2)
        off = lax.rem(t, 2) * (nz - 2 * k) + k
        z = lax.rem(at.z + off, nz)
        return z, (at.i, at.feat(at.xh, z, at.core))

    def loop(start, stop, body):
        lax.fori_loop(start, stop, lambda t, carry: (body(t), carry)[1], 0)

    tile_copy = pltpu.make_async_copy(tiles_ref, tiles, tile_sem)
    loads = [
        pltpu.make_async_copy(src, dst, load_sem.at[k])
        for k, (src, dst) in enumerate(
            [
                (rows_ref, rows),
                (cols_ref, cols),
                (live_ref, live),
                (weight_in, weight_ref),
                (x_ref, x_all.at[at.i]),
                (c_ref, c_all.at[at.j]),
            ]
        )
    ]
    for load in loads:
        load.start()
    tile_copy.start()
    greet([sibling, across, beside] + along_z + along_y)

    half_z, half_y = nz // 2, ny // 2

    def last_z(s, d):
        return half_z if s == d else nz - 1 - half_z

    def last_y(s, d):
        return half_y if s == d else ny - 1 - half_y

    def origin(place, count, d, t):
        return lax.rem(place + (count - t if d == 0 else t), count)

    def xh_of(s):
        return at.xh if s == 0 else 1 - at.xh

    def xl_of(s):
        return at.xl if s == 0 else 1 - at.xl

    def gz_copy(s, d, t, origin_z):
        block = c_all.at[at.feat(xh_of(s), origin_z, at.core)]
        src = c_ref if (s == 0 and t == 1) else block
        return remote(src, block, gzs.at[s, d, t - 1], gzr.at[s, d, t - 1], along_z[d])

    def sibling_copy(s, origin_z, src=None, arriving=False):
        core = 1 - at.core if arriving else at.core
        block = c_all.at[at.feat(xh_of(s), origin_z, core)]
        k = s * nz + origin_z
        return remote(block if src is None else src, block, gcs.at[k], gcr.at[k], sibling)

    def gy_copy(s, d, t, origin_y):
        block = x_all.at[at.node(origin_y, xl_of(s))]
        src = x_ref if (s == 0 and t == 1) else block
        return remote(src, block, gys.at[s, d, t - 1], gyr.at[s, d, t - 1], along_y[d])

    z_sent, y_sent = [], []

    def z_start(s, d, t):
        copy = gz_copy(s, d, t, origin(at.z, nz, d, t - 1))
        copy.start()
        z_sent.append(copy)

    def y_start(s, d, t):
        copy = gy_copy(s, d, t, origin(at.y, ny, d, t - 1))
        copy.start()
        y_sent.append(copy)

    def across_copy(xh):
        return remote(c_ref, c_all.at[at.feat(xh, at.z, at.core)], gxs, gxr, across)

    def beside_copy(xl):
        return remote(x_ref, x_all.at[at.node(at.y, xl)], gls, glr, beside)

    across_copy(at.xh).start()
    beside_copy(at.xl).start()
    for d in (0, 1):
        z_start(0, d, 1)
        y_start(0, d, 1)
    sent_over = [sibling_copy(0, at.z, c_ref)]
    sent_over[0].start()
    for load in loads:
        load.wait()
    spread_chains(rows, cols, live[0], n_feat, n_nodes, row_mat, col_mat, chain)
    chain_copy = pltpu.make_async_copy(chain.at[pl.ds(0, slots)], index, load_sem.at[0])
    chain_copy.start()
    beside_copy(1 - at.xl).wait_recv()
    for d in (0, 1):
        y_start(1, d, 1)
    across_copy(1 - at.xh).wait_recv()
    for d in (0, 1):
        z_start(1, d, 1)
    copy = sibling_copy(1, at.z)
    copy.start()
    sent_over.append(copy)


    def y_arrive(t):
        for s in (0, 1):
            for d in (0, 1):
                if t <= last_y(s, d):
                    gy_copy(s, d, t, origin(at.y, ny, d, t)).wait_recv()
                    if t < last_y(s, d):
                        y_start(s, d, t + 1)

    def z_arrive(s, d, t):
        if t <= last_z(s, d):
            origin_z = origin(at.z, nz, d, t)
            gz_copy(s, d, t, origin_z).wait_recv()
            if t < last_z(s, d):
                z_start(s, d, t + 1)
            over = sibling_copy(s, origin_z)
            over.start()
            sent_over.append(over)

    ways = [(s, d) for s in (0, 1) for d in (0, 1)]
    split = max(1, half_z - 2)
    for t in range(1, max(split, half_y) + 1):
        if t <= half_y:
            y_arrive(t)
        if t <= split:
            for s, d in ways:
                z_arrive(s, d, t)

    def add_chain(sums, terms, before, k0):
        for u, term in enumerate(terms):
            prev = index[k0 + u, before]
            sums[k0 + u] = term + jnp.where(prev >= 0, sums[jnp.maximum(prev, 0)], 0.0)

    def ahead_step(g):
        terms = [
            jnp.dot(tiles[g * GROUP + u], x_all[cols[g * GROUP + u]], preferred_element_type=jnp.float32)
            for u in range(GROUP)
        ]
        add_chain(ahead, terms, 0, g * GROUP)

    def back_step(g):
        terms = [
            lax.dot_general(
                tiles[g * GROUP + u], c_all[rows[g * GROUP + u]], (((0,), (0,)), ((), ())),
                preferred_element_type=jnp.float32,
            )
            for u in range(GROUP)
        ]
        add_chain(back, terms, 1, g * GROUP)

    def own_p(xh, z, core):
        k = index[at.feat(xh, z, core), 2]
        return jnp.where(k >= 0, ahead[jnp.maximum(k, 0)], 0.0)

    def own_b(y, xl):
        k = index[at.node(y, xl), 3]
        return jnp.where(k >= 0, back[jnp.maximum(k, 0)], 0.0)

    groups = slots // GROUP
    tile_copy.wait()
    chain_copy.wait()
    done = 0
    rest = [(s, d, t) for t in range(split + 1, half_z) for s, d in ways]
    for n, (s, d, t) in enumerate(rest):
        z_arrive(s, d, t)
        upto = groups * (n + 1) // len(rest)
        loop(done, upto, ahead_step)
        done = upto
    loop(done, groups, ahead_step)

    def c_copy(xh, z):
        slot = xh * nz + z
        return remote(p_tx.at[slot], c_rx.at[slot], cs.at[slot], cr.at[slot], sibling)

    def c_step(xh, z):
        p_tx[xh * nz + z] = own_p(xh, z, 1 - at.core).astype(jnp.bfloat16)
        c_copy(xh, z).start()

    loop(0, nz - 1, lambda t: c_step(1 - at.xh, z_peer(t)[0]))
    c_step(1 - at.xh, at.z)
    for s, d in ways:
        z_arrive(s, d, half_z)
    loop(0, nz - 1, lambda t: c_step(at.xh, z_peer(t)[0]))
    c_step(at.xh, at.z)

    def x_copy(z):
        return remote(x_tx.at[z], x_rx.at[z], xs.at[z], xr.at[z], across)

    def x_step(z):
        c_copy(1 - at.xh, z).wait_recv()
        x_tx[z] = (own_p(1 - at.xh, z, at.core) + wide(c_rx[(1 - at.xh) * nz + z])).astype(jnp.bfloat16)
        x_copy(z).start()

    loop(0, nz - 1, lambda t: x_step(z_peer(t)[0]))
    x_step(at.z)

    for s in (0, 1):
        for z in range(nz):
            sibling_copy(s, z, arriving=True).wait_recv()
    loop(0, groups, back_step)
    total = None
    for i in range(n_nodes):
        b_tx[i] = own_b(i // PAIR, i % PAIR).astype(jnp.bfloat16)
        term = lax.dot_general(x_all[i], b_tx[i], (((0,), (0,)), ((), ())), preferred_element_type=jnp.float32)
        total = term if total is None else total + term
    w0[...] = total.astype(w0.dtype).reshape(w0.shape)

    def w1_copy(t):
        i, device = node_peer(t)
        return remote(w0.at[i], w1.at[at.i], w1s.at[i], w1r.at[at.i], device)

    loop(1, n_nodes, lambda t: w1_copy(t).start())

    def y_copy(t):
        y, device = y_peer(t)
        return remote(b_tx.at[pl.ds(y * PAIR, PAIR)], y_rx.at[at.y], ys.at[y], yr.at[at.y], device)

    loop(1, ny, lambda t: y_copy(t).start())

    def z_copy(t):
        z, device = z_peer(t)
        return remote(z_tx.at[z], z_rx.at[at.z], zs.at[z], zr.at[at.z], device)

    def four_sum(z):
        c_copy(at.xh, z).wait_recv()
        x_copy(z).wait_recv()
        return own_p(at.xh, z, at.core) + wide(c_rx[at.xh * nz + z]) + wide(x_rx[z])

    def z_step(t):
        z = z_peer(t)[0]
        z_tx[z] = four_sum(z).astype(jnp.bfloat16)
        z_copy(t).start()

    first, second = nz // 3, 2 * nz // 3
    loop(0, first, z_step)

    def w1_arrival(t):
        i, device = node_peer(t)
        remote(w0.at[i], w1.at[i], w1s.at[i], w1r.at[i], device).wait_recv()

    w1[at.i] = w0[at.i]
    loop(1, n_nodes, w1_arrival)
    me4 = at.xh * 2 + at.core
    shared = jnp.sum(wide(w1[...]), axis=0)
    for slot in range(4):
        row, column = slot // 2 * 8, slot % 2 * 128
        w4_tx[slot] = shared[row : row + 8, column : column + 128]
    w4[me4] = w4_tx[me4]
    four = [
        (at.xh * 2 + 1 - at.core, sibling),
        ((1 - at.xh) * 2 + at.core, across),
        ((1 - at.xh) * 2 + 1 - at.core, slanted),
    ]

    def w4_copy(slot, device):
        return remote(w4_tx.at[slot], w4.at[me4], w4s.at[slot], w4r.at[me4], device)

    for slot, device in four:
        w4_copy(slot, device).start()
    loop(first, second, z_step)

    for slot, device in four:
        remote(w4_tx.at[slot], w4.at[slot], w4s.at[slot], w4r.at[slot], device).wait_recv()
    wz[at.z] = jnp.sum(w4[...], axis=0)

    def wz_copy(t):
        z, device = z_peer(t)
        return remote(wz.at[at.z], wz.at[at.z], wzs.at[z], wzr.at[at.z], device)

    loop(0, nz - 1, lambda t: wz_copy(t).start())
    loop(second, nz - 1, z_step)
    mine = four_sum(at.z)

    def wz_arrival(t):
        z, device = z_peer(t)
        remote(wz.at[z], wz.at[z], wzs.at[z], wzr.at[z], device).wait_recv()

    loop(0, nz - 1, wz_arrival)
    w5[me4] = jnp.sum(wz[...], axis=0) * scale

    def w5_copy(slot, device):
        return remote(w5.at[me4], w5.at[me4], w5s.at[slot], w5r.at[me4], device)

    for slot, device in four:
        w5_copy(slot, device).start()
    for slot, device in four:
        remote(w5.at[slot], w5.at[slot], w5s.at[slot], w5r.at[slot], device).wait_recv()
    wn[at.i] = jnp.concatenate(
        [jnp.concatenate([w5[2 * half], w5[2 * half + 1]], axis=1) for half in (0, 1)], axis=0
    ).astype(wn.dtype)

    def wn_copy(t):
        i, device = node_peer(t)
        return remote(wn.at[at.i], wn.at[at.i], wns.at[i], wnr.at[at.i], device)

    loop(1, n_nodes, lambda t: wn_copy(t).start())

    def y_arrival(t):
        y, device = y_peer(t)
        remote(b_tx.at[pl.ds(y * PAIR, PAIR)], y_rx.at[y], ys.at[y], yr.at[y], device).wait_recv()

    loop(1, ny, y_arrival)

    def y_sum(xl):
        def add(t, total):
            return total + wide(y_rx[y_peer(t)[0], xl])

        return lax.fori_loop(1, ny, add, own_b(at.y, xl))

    l_copy = remote(l_tx, l_rx, ls, lr, beside)
    l_tx[...] = y_sum(1 - at.xl).astype(jnp.bfloat16)
    l_copy.start()
    near = y_sum(at.xl)

    def z_arrival(t, total):
        z, device = z_peer(t)
        remote(z_tx.at[z], z_rx.at[z], zs.at[z], zr.at[z], device).wait_recv()
        return total + wide(z_rx[z])

    whole = lax.fori_loop(0, nz - 1, z_arrival, mine)
    out_ref[...] = split_dot(whole, weight_ref[...], ((1,), (0,))).astype(out_ref.dtype)

    l_copy.wait_recv()
    fg_ref[...] = split_dot(near + wide(l_rx[...]), weight_ref[...], ((1,), (1,))).astype(fg_ref.dtype)

    def wn_arrival(t):
        i, device = node_peer(t)
        remote(wn.at[i], wn.at[i], wns.at[i], wnr.at[i], device).wait_recv()

    loop(1, n_nodes, wn_arrival)
    wg_ref[...] = wide(wn[...])

    for sent in sent_over + z_sent + y_sent:
        sent.wait_send()
    across_copy(at.xh).wait_send()
    beside_copy(at.xl).wait_send()
    for xh in (0, 1):
        loop(0, nz, lambda z: c_copy(xh, z).wait_send())
    loop(0, nz, lambda z: x_copy(z).wait_send())
    loop(1, n_nodes, lambda t: w1_copy(t).wait_send())
    loop(1, ny, lambda t: y_copy(t).wait_send())
    loop(0, nz - 1, lambda t: z_copy(t).wait_send())
    for slot, device in four:
        w4_copy(slot, device).wait_send()
        w5_copy(slot, device).wait_send()
    loop(0, nz - 1, lambda t: wz_copy(t).wait_send())
    l_copy.wait_send()
    loop(1, n_nodes, lambda t: wn_copy(t).wait_send())


def body(n_nodes, n_feat, features, weight, tiles, tile_rows, tile_cols, live, cotangent):
    rows, width = features.shape
    scale = 1.0 / math.sqrt(rows * n_nodes * n_feat)
    ny, nz = n_nodes // PAIR, n_feat // (PAIR * PAIR)
    slots, side = tiles.shape[:2]
    share = width // n_nodes
    dma = pltpu.SemaphoreType.DMA

    def blocks(*lead, kind=jnp.bfloat16):
        return pltpu.VMEM((*lead, rows, width), kind)

    def shares(count, kind):
        return pltpu.VMEM((count, share, width), kind)

    def pieces(count):
        return pltpu.VMEM((count, share // 2, width // 2), jnp.float32)

    def pairs(*counts):
        return [sem for count in counts for sem in [dma(count) if count else dma] * 2]

    output, feature_grad, weight_grad = pl.pallas_call(
        functools.partial(kernel, n_nodes, n_feat, scale),
        out_shape=(
            jax.ShapeDtypeStruct((rows, width), jnp.bfloat16),
            jax.ShapeDtypeStruct((rows, width), jnp.bfloat16),
            jax.ShapeDtypeStruct((n_nodes, share, width), jnp.float32),
        ),
        in_specs=[ANY] * 7,
        out_specs=(VMEM,) * 3,
        scratch_shapes=[
            pltpu.SMEM(tile_rows.shape, jnp.int32),
            pltpu.SMEM(tile_cols.shape, jnp.int32),
            pltpu.SMEM(live.shape, jnp.int32),
            pltpu.VMEM((LANES, LANES), jnp.int32),
            pltpu.VMEM((LANES, LANES), jnp.int32),
            pltpu.VMEM((LANES, LANES), jnp.int32),
            pltpu.SMEM((slots, LANES), jnp.int32),
            pltpu.VMEM(weight.shape, weight.dtype),
            pltpu.VMEM(tiles.shape, tiles.dtype),
            blocks(n_nodes),
            blocks(n_feat),
            blocks(slots, kind=jnp.float32),
            blocks(slots, kind=jnp.float32),
            blocks(2 * nz),
            blocks(n_nodes),
            blocks(2 * nz),
            blocks(nz),
            blocks(nz),
            blocks(nz),
            blocks(nz),
            blocks(ny, PAIR),
            blocks(),
            blocks(),
            shares(n_nodes, jnp.bfloat16),
            shares(n_nodes, jnp.bfloat16),
            pieces(4),
            pieces(4),
            pieces(nz),
            pieces(4),
            shares(n_nodes, jnp.bfloat16),
            dma((6,)),
            dma,
        ]
        + pairs(None, (2, 2, nz // 2), (2 * nz,), None, (2, 2, ny // 2))
        + pairs((2 * nz,), (nz,), (nz,), (ny,), None)
        + pairs((n_nodes,), (4,), (nz,), (4,), (n_nodes,)),
        compiler_params=pltpu.CompilerParams(collective_id=0, has_side_effects=True, vmem_limit_bytes=LIMIT),
        name="graph_layer",
    )(tile_rows, tile_cols, live, features, cotangent, weight, tiles)
    return output, feature_grad, weight_grad.reshape(weight.shape)


def solution(mesh):
    in_specs = (
        P(("feat", "nodes"), None),
        P(),
        P(("nodes", "feat"), None, None),
        P(("nodes", "feat")),
        P(("nodes", "feat")),
        P(("nodes", "feat")),
        P(("nodes", "feat"), None),
    )
    out_specs = (P(("nodes", "feat"), None), P(("feat", "nodes"), None), P())
    step = functools.partial(body, mesh.shape["nodes"], mesh.shape["feat"])
    return jax.shard_map(step, mesh=mesh, in_specs=in_specs, out_specs=out_specs, check_vma=False)
```

```python
import functools
import math

import jax
import jax.numpy as jnp
from jax import lax
from jax.experimental import pallas as pl
from jax.experimental.pallas import tpu as pltpu
from jax.sharding import PartitionSpec as P

MESH = pl.DeviceIdType.MESH
VMEM = pl.BlockSpec(memory_space=pltpu.VMEM)
ANY = pl.BlockSpec(memory_space=pl.ANY)
LIMIT = 60 * 1024 * 1024
LANES = 128
GROUP = 4
PAIR = 2


class Place:
    def __init__(self, n_nodes, n_feat):
        self.n_nodes, self.n_feat = n_nodes, n_feat
        self.ny, self.nz = n_nodes // PAIR, n_feat // (PAIR * PAIR)
        self.i, self.j = lax.axis_index("nodes"), lax.axis_index("feat")
        self.y, self.xl = lax.div(self.i, PAIR), lax.rem(self.i, PAIR)
        self.xh = lax.div(self.j, PAIR * self.nz)
        self.z = lax.rem(lax.div(self.j, PAIR), self.nz)
        self.core = lax.rem(self.j, PAIR)

    def node(self, y, xl):
        return y * PAIR + xl

    def feat(self, xh, z, core):
        return (xh * self.nz + z) * PAIR + core


def greet(partners):
    barrier = pltpu.get_barrier_semaphore()
    for device in partners:
        pl.semaphore_signal(barrier, inc=1, device_id=device, device_id_type=MESH)
    pl.semaphore_wait(barrier, len(partners))


def remote(src, dst, send_sem, recv_sem, device):
    return pltpu.make_async_remote_copy(
        src_ref=src, dst_ref=dst, send_sem=send_sem, recv_sem=recv_sem, device_id=device, device_id_type=MESH
    )


def wide(value):
    return value.astype(jnp.float32)


def split_dot(value, weight, dims):
    high = value.astype(jnp.bfloat16)
    low = (value - wide(high)).astype(jnp.bfloat16)
    return sum(
        lax.dot_general(part, weight, (dims, ((), ())), preferred_element_type=jnp.float32) for part in (high, low)
    )


def spread_chains(rows, cols, live, row_count, col_count, row_mat, col_mat, chain):
    slots = rows.shape[0]

    def fill(k, carry):
        row_mat[pl.ds(k, 1), :] = jnp.full((1, LANES), rows[k], jnp.int32)
        col_mat[pl.ds(k, 1), :] = jnp.full((1, LANES), cols[k], jnp.int32)
        return carry

    row_mat[...] = jnp.full(row_mat.shape, -1, jnp.int32)
    col_mat[...] = jnp.full(col_mat.shape, -1, jnp.int32)
    lax.fori_loop(0, slots, fill, 0)
    line = lax.broadcasted_iota(jnp.int32, (LANES, LANES), 0)
    slot = lax.broadcasted_iota(jnp.int32, (LANES, LANES), 1)

    def best(keep):
        return jnp.max(jnp.where(keep, slot, -1), axis=1, keepdims=True)

    found = []
    for mat in (row_mat, col_mat):
        along, across = mat[...], mat[...].T
        found.append((best((along == across) & (slot < line)), best((across == line) & (slot < live))))
    (before_row, last_row), (before_col, last_col) = found
    chain[...] = jnp.where(
        slot == 0, before_row, jnp.where(slot == 1, before_col, jnp.where(slot == 2, last_row, last_col))
    )


def kernel(
    n_nodes, n_feat, scale,
    rows_ref, cols_ref, live_ref, x_ref, c_ref, weight_in, tiles_ref, out_ref, fg_ref, wg_ref,
    rows, cols, live, row_mat, col_mat, chain, index, weight_ref, tiles, x_all, c_all, ahead, back, p_tx, c_rx, x_tx, x_rx, rz_tx, rz_rx, rz_tx32, rz_rx32, ry_tx, ry_rx, l_tx, l_rx,
    b_all, w0, w1, w4, wz, wn, load_sem, tile_sem,
    gxs, gxr, gzs, gzr, gcs, gcr, gls, glr, gys, gyr,
    cs, cr, xs, xr, rzs, rzr, rys, ryr, ls, lr, w1s, w1r, w4s, w4r, wzs, wzr, wns, wnr,
):
    at = Place(n_nodes, n_feat)
    nz, ny = at.nz, at.ny
    slots = tiles.shape[0]
    z_near = [lax.rem(at.z + 1, nz), lax.rem(at.z + nz - 1, nz)]
    y_near = [lax.rem(at.y + 1, ny), lax.rem(at.y + ny - 1, ny)]
    sibling = (at.i, at.feat(at.xh, at.z, 1 - at.core))
    across = (at.i, at.feat(1 - at.xh, at.z, at.core))
    slanted = (at.i, at.feat(1 - at.xh, at.z, 1 - at.core))
    beside = (at.node(at.y, 1 - at.xl), at.j)
    along_z = [(at.i, at.feat(at.xh, z, at.core)) for z in z_near]
    along_y = [(at.node(y, at.xl), at.j) for y in y_near]

    def node_peer(t):
        i = lax.rem(at.i + t, n_nodes)
        return i, (i, at.j)

    def z_peer(t):
        k = lax.div(nz - 1 - t, 2) + lax.rem(nz - 1 - t, 2)
        off = lax.rem(t, 2) * (nz - 2 * k) + k
        z = lax.rem(at.z + off, nz)
        return z, (at.i, at.feat(at.xh, z, at.core))

    def loop(start, stop, body):
        lax.fori_loop(start, stop, lambda t, carry: (body(t), carry)[1], 0)

    tile_copy = pltpu.make_async_copy(tiles_ref, tiles, tile_sem)
    loads = [
        pltpu.make_async_copy(src, dst, load_sem.at[k])
        for k, (src, dst) in enumerate(
            [
                (rows_ref, rows),
                (cols_ref, cols),
                (live_ref, live),
                (weight_in, weight_ref),
                (x_ref, x_all.at[at.i]),
                (c_ref, c_all.at[at.j]),
            ]
        )
    ]
    for load in loads:
        load.start()
    tile_copy.start()
    greet([sibling, across, beside] + along_z + along_y)

    half_z, half_y = nz // 2, ny // 2

    def last_z(s, d):
        return half_z if s == d else nz - 1 - half_z

    def last_y(s, d):
        return half_y if s == d else ny - 1 - half_y

    def origin(place, count, d, t):
        return lax.rem(place + (count - t if d == 0 else t), count)

    def xh_of(s):
        return at.xh if s == 0 else 1 - at.xh

    def xl_of(s):
        return at.xl if s == 0 else 1 - at.xl

    def gz_copy(s, d, t, origin_z):
        block = c_all.at[at.feat(xh_of(s), origin_z, at.core)]
        src = c_ref if (s == 0 and t == 1) else block
        return remote(src, block, gzs.at[s, d, t - 1], gzr.at[s, d, t - 1], along_z[d])

    def sibling_copy(s, origin_z, src=None, arriving=False):
        core = 1 - at.core if arriving else at.core
        block = c_all.at[at.feat(xh_of(s), origin_z, core)]
        k = s * nz + origin_z
        return remote(block if src is None else src, block, gcs.at[k], gcr.at[k], sibling)

    def gy_copy(s, d, t, origin_y):
        block = x_all.at[at.node(origin_y, xl_of(s))]
        src = x_ref if (s == 0 and t == 1) else block
        return remote(src, block, gys.at[s, d, t - 1], gyr.at[s, d, t - 1], along_y[d])

    z_sent, y_sent = [], []

    def z_start(s, d, t):
        copy = gz_copy(s, d, t, origin(at.z, nz, d, t - 1))
        copy.start()
        z_sent.append(copy)

    def y_start(s, d, t):
        copy = gy_copy(s, d, t, origin(at.y, ny, d, t - 1))
        copy.start()
        y_sent.append(copy)

    def across_copy(xh):
        return remote(c_ref, c_all.at[at.feat(xh, at.z, at.core)], gxs, gxr, across)

    def beside_copy(xl):
        return remote(x_ref, x_all.at[at.node(at.y, xl)], gls, glr, beside)

    across_copy(at.xh).start()
    beside_copy(at.xl).start()
    for d in (0, 1):
        z_start(0, d, 1)
        y_start(0, d, 1)
    sent_over = [sibling_copy(0, at.z, c_ref)]
    sent_over[0].start()
    def y_arrive(s, t):
        for d in (0, 1):
            if t <= last_y(s, d):
                gy_copy(s, d, t, origin(at.y, ny, d, t)).wait_recv()
                if t < last_y(s, d):
                    y_start(s, d, t + 1)

    def z_arrive(s, d, t):
        origin_z = origin(at.z, nz, d, t)
        gz_copy(s, d, t, origin_z).wait_recv()
        if t < last_z(s, d):
            z_start(s, d, t + 1)
        return sibling_copy(s, origin_z)

    ways = [(s, d) for s in (0, 1) for d in (0, 1)]

    def order(count):
        steps = [(0, 1), (0, 2)]
        for t in range(1, count + 1):
            steps += [(1, t), (0, t + 2)]
        return [(s, t) for s, t in steps if t <= count]

    z_order = [(s, d, t) for s, t in order(half_z) for d in (0, 1) if t <= last_z(s, d)]
    y_order = order(half_y)

    def z_next(count):
        over = [z_arrive(*z_order.pop(0)) for _ in range(min(count, len(z_order)))]
        for copy in over:
            copy.start()
        sent_over.extend(over)

    z_next(2)
    y_arrive(*y_order.pop(0))
    across_copy(1 - at.xh).wait_recv()
    for d in (0, 1):
        z_start(1, d, 1)
    partners = sibling_copy(1, at.z)
    partners.start()
    sent_over.append(partners)
    beside_copy(1 - at.xl).wait_recv()
    for d in (0, 1):
        y_start(1, d, 1)
    for load in loads:
        load.wait()
    spread_chains(rows, cols, live[0], n_feat, n_nodes, row_mat, col_mat, chain)
    chain_copy = pltpu.make_async_copy(chain.at[pl.ds(0, slots)], index, load_sem.at[0])
    chain_copy.start()
    while y_order:
        if len(y_order) > 1:
            z_next(2)
        y_arrive(*y_order.pop(0))

    def add_chain(sums, terms, before, k0):
        for u, term in enumerate(terms):
            prev = index[k0 + u, before]
            sums[k0 + u] = term + jnp.where(prev >= 0, sums[jnp.maximum(prev, 0)], 0.0)

    def ahead_step(g):
        terms = [
            jnp.dot(tiles[g * GROUP + u], x_all[cols[g * GROUP + u]], preferred_element_type=jnp.float32)
            for u in range(GROUP)
        ]
        add_chain(ahead, terms, 0, g * GROUP)

    def back_step(g):
        terms = [
            lax.dot_general(
                tiles[g * GROUP + u], c_all[rows[g * GROUP + u]], (((0,), (0,)), ((), ())),
                preferred_element_type=jnp.float32,
            )
            for u in range(GROUP)
        ]
        add_chain(back, terms, 1, g * GROUP)

    def own_p(xh, z, core):
        k = index[at.feat(xh, z, core), 2]
        return jnp.where(k >= 0, ahead[jnp.maximum(k, 0)], 0.0)

    def own_b(y, xl):
        k = index[at.node(y, xl), 3]
        return jnp.where(k >= 0, back[jnp.maximum(k, 0)], 0.0)

    groups = slots // GROUP
    tile_copy.wait()
    chain_copy.wait()
    parts = 2
    for part in range(parts):
        z_next(1)
        loop(groups * part // parts, groups * (part + 1) // parts, ahead_step)

    def c_copy(xh, z):
        slot = xh * nz + z
        return remote(p_tx.at[slot], c_rx.at[slot], cs.at[slot], cr.at[slot], sibling)

    def c_step(xh, z):
        p_tx[xh * nz + z] = own_p(xh, z, 1 - at.core).astype(jnp.bfloat16)
        c_copy(xh, z).start()

    for part in range(parts):
        first, end = nz * part // parts, nz * (part + 1) // parts
        loop(first, min(end, nz - 1), lambda t: c_step(1 - at.xh, z_peer(t)[0]))
        z_next(1)
    c_step(1 - at.xh, at.z)

    def x_copy(z):
        return remote(x_tx.at[z], x_rx.at[z], xs.at[z], xr.at[z], across)

    def x_step(z):
        c_copy(1 - at.xh, z).wait_recv()
        x_tx[z] = (own_p(1 - at.xh, z, at.core) + wide(c_rx[(1 - at.xh) * nz + z])).astype(jnp.bfloat16)
        x_copy(z).start()

    parts = len(z_order)
    for part in range(parts):
        first, end = nz * part // parts, nz * (part + 1) // parts
        loop(first, min(end, nz - 1), lambda t: x_step(z_peer(t)[0]))
        z_next(1)
    x_step(at.z)
    loop(0, nz - 1, lambda t: c_step(at.xh, z_peer(t)[0]))
    c_step(at.xh, at.z)

    for s in (0, 1):
        for z in range(nz):
            sibling_copy(s, z, arriving=True).wait_recv()
    loop(0, groups, back_step)

    def round_b(t):
        b_all[t] = own_b(lax.div(t, PAIR), lax.rem(t, PAIR)).astype(jnp.bfloat16)

    loop(0, n_nodes, round_b)
    width = x_all.shape[-1]
    term = lax.dot_general(
        x_all[...].reshape(-1, width), b_all[...].reshape(-1, width), (((0,), (0,)), ((), ())),
        preferred_element_type=jnp.float32,
    )
    w0[...] = term.astype(w0.dtype).reshape(w0.shape)

    def w1_copy(t):
        i, device = node_peer(t)
        return remote(w0.at[i], w1.at[at.i], w1s.at[i], w1r.at[at.i], device)

    loop(1, n_nodes, lambda t: w1_copy(t).start())

    def y_hops(d, s):
        return half_y if d == s else ny - 1 - half_y

    def ry_copy(d, s, h):
        return remote(ry_tx.at[d, s, h - 1], ry_rx.at[d, s, h - 1], rys.at[d, s, h - 1], ryr.at[d, s, h - 1], along_y[d])

    def y_hop(h):
        for d, s in ways:
            hops = y_hops(d, s)
            if h <= hops:
                value = own_b(origin(at.y, ny, 1 - d, hops + 1 - h), xl_of(s))
                if h > 1:
                    ry_copy(d, s, h - 1).wait_recv()
                    value = value + wide(ry_rx[d, s, h - 2])
                ry_tx[d, s, h - 1] = value.astype(jnp.bfloat16)
                ry_copy(d, s, h).start()

    def y_sum(s):
        value = own_b(at.y, xl_of(s))
        for d in (0, 1):
            hops = y_hops(d, s)
            ry_copy(d, s, hops).wait_recv()
            value = value + wide(ry_rx[d, s, hops - 1])
        return value

    z_hops = (half_z, nz - 1 - half_z)

    def rz_refs(d, h):
        late = h - (z_hops[d] - 1)
        return (rz_tx32.at[d, late], rz_rx32.at[d, late]) if late >= 0 else (rz_tx.at[d, h - 1], rz_rx.at[d, h - 1])

    def rz_copy(d, h):
        return remote(*rz_refs(d, h), rzs.at[d, h - 1], rzr.at[d, h - 1], along_z[d])

    def four_sum(z):
        c_copy(at.xh, z).wait_recv()
        x_copy(z).wait_recv()
        return own_p(at.xh, z, at.core) + wide(c_rx[at.xh * nz + z]) + wide(x_rx[z])

    def z_hop(h):
        for d in (0, 1):
            hops = z_hops[d]
            if h <= hops:
                value = four_sum(origin(at.z, nz, 1 - d, hops + 1 - h))
                if h > 1:
                    rz_copy(d, h - 1).wait_recv()
                    value = value + wide(rz_refs(d, h - 1)[1][...])
                tx = rz_refs(d, h)[0]
                tx[...] = value.astype(tx.dtype)
                rz_copy(d, h).start()

    y_hop(1)
    z_hop(1)
    z_hop(2)
    y_hop(2)
    z_hop(3)

    def w1_arrival(t):
        i, device = node_peer(t)
        remote(w0.at[i], w1.at[i], w1s.at[i], w1r.at[i], device).wait_recv()

    w1[at.i] = w0[at.i]
    loop(1, n_nodes, w1_arrival)
    me4 = at.xh * 2 + at.core
    w4[me4] = jnp.sum(wide(w1[...]), axis=0)
    four = [
        (at.xh * 2 + 1 - at.core, sibling),
        ((1 - at.xh) * 2 + at.core, across),
        ((1 - at.xh) * 2 + 1 - at.core, slanted),
    ]

    def w4_copy(slot, device):
        return remote(w4.at[me4], w4.at[me4], w4s.at[slot], w4r.at[me4], device)

    for slot, device in four:
        w4_copy(slot, device).start()
    z_hop(4)
    y_hop(3)

    for slot, device in four:
        remote(w4.at[slot], w4.at[slot], w4s.at[slot], w4r.at[slot], device).wait_recv()
    wz[at.z] = jnp.sum(w4[...], axis=0).astype(wz.dtype)

    def wz_copy(t):
        z, device = z_peer(t)
        return remote(wz.at[at.z], wz.at[at.z], wzs.at[z], wzr.at[at.z], device)

    loop(0, nz - 1, lambda t: wz_copy(t).start())
    z_hop(5)
    y_hop(4)
    z_hop(6)

    def wz_arrival(t):
        z, device = z_peer(t)
        remote(wz.at[z], wz.at[z], wzs.at[z], wzr.at[z], device).wait_recv()

    loop(0, nz - 1, wz_arrival)
    wn[at.i] = (jnp.sum(wide(wz[...]), axis=0) * scale).astype(wn.dtype)

    def wn_copy(t):
        i, device = node_peer(t)
        return remote(wn.at[at.i], wn.at[at.i], wns.at[i], wnr.at[at.i], device)

    loop(1, n_nodes, lambda t: wn_copy(t).start())
    l_copy = remote(l_tx, l_rx, ls, lr, beside)
    l_tx[...] = y_sum(1).astype(jnp.bfloat16)
    l_copy.start()
    near = y_sum(0)
    l_copy.wait_recv()
    fg_ref[...] = split_dot(near + wide(l_rx[...]), weight_ref[...], ((1,), (1,))).astype(fg_ref.dtype)

    whole = four_sum(at.z)
    for d in (0, 1):
        rz_copy(d, z_hops[d]).wait_recv()
        whole = whole + wide(rz_refs(d, z_hops[d])[1][...])
    out_ref[...] = split_dot(whole, weight_ref[...], ((1,), (0,))).astype(out_ref.dtype)

    def wn_arrival(t):
        i, device = node_peer(t)
        remote(wn.at[i], wn.at[i], wns.at[i], wnr.at[i], device).wait_recv()

    loop(1, n_nodes, wn_arrival)
    wg_ref[...] = wide(wn[...])

    for sent in sent_over + z_sent + y_sent:
        sent.wait_send()
    across_copy(at.xh).wait_send()
    beside_copy(at.xl).wait_send()
    for xh in (0, 1):
        loop(0, nz, lambda z: c_copy(xh, z).wait_send())
    loop(0, nz, lambda z: x_copy(z).wait_send())
    loop(1, n_nodes, lambda t: w1_copy(t).wait_send())
    for d, s in ways:
        for h in range(1, y_hops(d, s) + 1):
            ry_copy(d, s, h).wait_send()
    for d in (0, 1):
        for h in range(1, z_hops[d] + 1):
            rz_copy(d, h).wait_send()
    for slot, device in four:
        w4_copy(slot, device).wait_send()
    loop(0, nz - 1, lambda t: wz_copy(t).wait_send())
    l_copy.wait_send()
    loop(1, n_nodes, lambda t: wn_copy(t).wait_send())


def body(n_nodes, n_feat, features, weight, tiles, tile_rows, tile_cols, live, cotangent):
    rows, width = features.shape
    scale = 1.0 / math.sqrt(rows * n_nodes * n_feat)
    ny, nz = n_nodes // PAIR, n_feat // (PAIR * PAIR)
    slots, side = tiles.shape[:2]
    share = width // n_nodes
    dma = pltpu.SemaphoreType.DMA

    def blocks(*lead, kind=jnp.bfloat16):
        return pltpu.VMEM((*lead, rows, width), kind)

    def shares(count, kind):
        return pltpu.VMEM((count, share, width), kind)

    def pairs(*counts):
        return [sem for count in counts for sem in [dma(count) if count else dma] * 2]

    output, feature_grad, weight_grad = pl.pallas_call(
        functools.partial(kernel, n_nodes, n_feat, scale),
        out_shape=(
            jax.ShapeDtypeStruct((rows, width), jnp.bfloat16),
            jax.ShapeDtypeStruct((rows, width), jnp.bfloat16),
            jax.ShapeDtypeStruct((n_nodes, share, width), jnp.float32),
        ),
        in_specs=[ANY] * 7,
        out_specs=(VMEM,) * 3,
        scratch_shapes=[
            pltpu.SMEM(tile_rows.shape, jnp.int32),
            pltpu.SMEM(tile_cols.shape, jnp.int32),
            pltpu.SMEM(live.shape, jnp.int32),
            pltpu.VMEM((LANES, LANES), jnp.int32),
            pltpu.VMEM((LANES, LANES), jnp.int32),
            pltpu.VMEM((LANES, LANES), jnp.int32),
            pltpu.SMEM((slots, LANES), jnp.int32),
            pltpu.VMEM(weight.shape, weight.dtype),
            pltpu.VMEM(tiles.shape, tiles.dtype),
            blocks(n_nodes),
            blocks(n_feat),
            blocks(slots, kind=jnp.float32),
            blocks(slots, kind=jnp.float32),
            blocks(2 * nz),
            blocks(2 * nz),
            blocks(nz),
            blocks(nz),
            blocks(2, nz // 2),
            blocks(2, nz // 2),
            blocks(2, 2, kind=jnp.float32),
            blocks(2, 2, kind=jnp.float32),
            blocks(2, 2, ny // 2),
            blocks(2, 2, ny // 2),
            blocks(),
            blocks(),
            blocks(n_nodes),
            shares(n_nodes, jnp.bfloat16),
            shares(n_nodes, jnp.bfloat16),
            shares(4, jnp.float32),
            shares(nz, jnp.bfloat16),
            shares(n_nodes, jnp.bfloat16),
            dma((6,)),
            dma,
        ]
        + pairs(None, (2, 2, nz // 2), (2 * nz,), None, (2, 2, ny // 2))
        + pairs((2 * nz,), (nz,), (2, nz // 2), (2, 2, ny // 2), None)
        + pairs((n_nodes,), (4,), (nz,), (n_nodes,)),
        compiler_params=pltpu.CompilerParams(collective_id=0, has_side_effects=True, vmem_limit_bytes=LIMIT),
        name="graph_layer",
    )(tile_rows, tile_cols, live, features, cotangent, weight, tiles)
    return output, feature_grad, weight_grad.reshape(weight.shape)


def solution(mesh):
    in_specs = (
        P(("feat", "nodes"), None),
        P(),
        P(("nodes", "feat"), None, None),
        P(("nodes", "feat")),
        P(("nodes", "feat")),
        P(("nodes", "feat")),
        P(("nodes", "feat"), None),
    )
    out_specs = (P(("nodes", "feat"), None), P(("feat", "nodes"), None), P())
    step = functools.partial(body, mesh.shape["nodes"], mesh.shape["feat"])
    return jax.shard_map(step, mesh=mesh, in_specs=in_specs, out_specs=out_specs, check_vma=False)
```

```python
import functools
import math

import jax
import jax.numpy as jnp
from jax import lax
from jax.experimental import pallas as pl
from jax.experimental.pallas import tpu as pltpu
from jax.sharding import PartitionSpec as P

MESH = pl.DeviceIdType.MESH
VMEM = pl.BlockSpec(memory_space=pltpu.VMEM)
ANY = pl.BlockSpec(memory_space=pl.ANY)
LIMIT = 60 * 1024 * 1024
LANES = 128
GROUP = 16
PAIR = 2


class Place:
    def __init__(self, n_nodes, n_feat):
        self.n_nodes, self.n_feat = n_nodes, n_feat
        self.ny, self.nz = n_nodes // PAIR, n_feat // (PAIR * PAIR)
        self.i, self.j = lax.axis_index("nodes"), lax.axis_index("feat")
        self.y, self.xl = lax.div(self.i, PAIR), lax.rem(self.i, PAIR)
        self.xh = lax.div(self.j, PAIR * self.nz)
        self.z = lax.rem(lax.div(self.j, PAIR), self.nz)
        self.core = lax.rem(self.j, PAIR)

    def node(self, y, xl):
        return y * PAIR + xl

    def feat(self, xh, z, core):
        return (xh * self.nz + z) * PAIR + core


def greet(partners):
    barrier = pltpu.get_barrier_semaphore()
    for device in partners:
        pl.semaphore_signal(barrier, inc=1, device_id=device, device_id_type=MESH)
    pl.semaphore_wait(barrier, len(partners))


def remote(src, dst, send_sem, recv_sem, device):
    return pltpu.make_async_remote_copy(
        src_ref=src, dst_ref=dst, send_sem=send_sem, recv_sem=recv_sem, device_id=device, device_id_type=MESH
    )


def wide(value):
    return value.astype(jnp.float32)


def split_dot(value, weight, dims):
    high = value.astype(jnp.bfloat16)
    low = (value - wide(high)).astype(jnp.bfloat16)
    return sum(
        lax.dot_general(part, weight, (dims, ((), ())), preferred_element_type=jnp.float32) for part in (high, low)
    )


def spread_chains(rows, cols, live, row_count, col_count, row_mat, col_mat, chain):
    slots = rows.shape[0]

    def fill(k, carry):
        row_mat[pl.ds(k, 1), :] = jnp.full((1, LANES), rows[k], jnp.int32)
        col_mat[pl.ds(k, 1), :] = jnp.full((1, LANES), cols[k], jnp.int32)
        return carry

    row_mat[...] = jnp.full(row_mat.shape, -1, jnp.int32)
    col_mat[...] = jnp.full(col_mat.shape, -1, jnp.int32)
    lax.fori_loop(0, slots, fill, 0)
    line = lax.broadcasted_iota(jnp.int32, (LANES, LANES), 0)
    slot = lax.broadcasted_iota(jnp.int32, (LANES, LANES), 1)

    def best(keep):
        return jnp.max(jnp.where(keep, slot, -1), axis=1, keepdims=True)

    found = []
    for mat in (row_mat, col_mat):
        along, across = mat[...], mat[...].T
        found.append((best((along == across) & (slot < line)), best((across == line) & (slot < live))))
    (before_row, last_row), (before_col, last_col) = found
    chain[...] = jnp.where(
        slot == 0, before_row, jnp.where(slot == 1, before_col, jnp.where(slot == 2, last_row, last_col))
    )


def kernel(
    n_nodes, n_feat, scale,
    rows_ref, cols_ref, live_ref, x_ref, c_ref, weight_in, tiles_ref, out_ref, fg_ref, wg_ref,
    rows, cols, live, row_mat, col_mat, chain, index, weight_ref, tiles, x_all, c_all, ahead, back, p_tx, c_rx, x_tx, x_rx, rz_tx, rz_rx, rz_tx32, rz_rx32, ry_tx, ry_rx, l_tx, l_rx,
    b_all, w0, w1, w4, wz, wn, load_sem, tile_sem,
    gxs, gxr, gzs, gzr, gcs, gcr, gls, glr, gys, gyr,
    cs, cr, xs, xr, rzs, rzr, rys, ryr, ls, lr, w1s, w1r, w4s, w4r, wzs, wzr, wns, wnr,
):
    at = Place(n_nodes, n_feat)
    nz, ny = at.nz, at.ny
    slots = tiles.shape[0]
    z_near = [lax.rem(at.z + 1, nz), lax.rem(at.z + nz - 1, nz)]
    y_near = [lax.rem(at.y + 1, ny), lax.rem(at.y + ny - 1, ny)]
    sibling = (at.i, at.feat(at.xh, at.z, 1 - at.core))
    across = (at.i, at.feat(1 - at.xh, at.z, at.core))
    slanted = (at.i, at.feat(1 - at.xh, at.z, 1 - at.core))
    beside = (at.node(at.y, 1 - at.xl), at.j)
    along_z = [(at.i, at.feat(at.xh, z, at.core)) for z in z_near]
    along_y = [(at.node(y, at.xl), at.j) for y in y_near]

    def node_peer(t):
        i = lax.rem(at.i + t, n_nodes)
        return i, (i, at.j)

    def z_peer(t):
        k = lax.div(nz - 1 - t, 2) + lax.rem(nz - 1 - t, 2)
        off = lax.rem(t, 2) * (nz - 2 * k) + k
        z = lax.rem(at.z + off, nz)
        return z, (at.i, at.feat(at.xh, z, at.core))

    def loop(start, stop, body):
        lax.fori_loop(start, stop, lambda t, carry: (body(t), carry)[1], 0)

    tile_copy = pltpu.make_async_copy(tiles_ref, tiles, tile_sem)
    loads = [
        pltpu.make_async_copy(src, dst, load_sem.at[k])
        for k, (src, dst) in enumerate(
            [
                (rows_ref, rows),
                (cols_ref, cols),
                (live_ref, live),
                (weight_in, weight_ref),
                (x_ref, x_all.at[at.i]),
                (c_ref, c_all.at[at.j]),
            ]
        )
    ]
    for load in loads:
        load.start()
    tile_copy.start()
    greet([sibling, across, beside] + along_z + along_y)

    half_z, half_y = nz // 2, ny // 2

    def last_z(s, d):
        return half_z if s == d else nz - 1 - half_z

    def last_y(s, d):
        return half_y if s == d else ny - 1 - half_y

    def origin(place, count, d, t):
        return lax.rem(place + (count - t if d == 0 else t), count)

    def xh_of(s):
        return at.xh if s == 0 else 1 - at.xh

    def xl_of(s):
        return at.xl if s == 0 else 1 - at.xl

    def gz_copy(s, d, t, origin_z):
        block = c_all.at[at.feat(xh_of(s), origin_z, at.core)]
        src = c_ref if (s == 0 and t == 1) else block
        return remote(src, block, gzs.at[s, d, t - 1], gzr.at[s, d, t - 1], along_z[d])

    def sibling_copy(s, origin_z, src=None, arriving=False):
        core = 1 - at.core if arriving else at.core
        block = c_all.at[at.feat(xh_of(s), origin_z, core)]
        k = s * nz + origin_z
        return remote(block if src is None else src, block, gcs.at[k], gcr.at[k], sibling)

    def gy_copy(s, d, t, origin_y):
        block = x_all.at[at.node(origin_y, xl_of(s))]
        src = x_ref if (s == 0 and t == 1) else block
        return remote(src, block, gys.at[s, d, t - 1], gyr.at[s, d, t - 1], along_y[d])

    z_sent, y_sent = [], []

    def z_start(s, d, t):
        copy = gz_copy(s, d, t, origin(at.z, nz, d, t - 1))
        copy.start()
        z_sent.append(copy)

    def y_start(s, d, t):
        copy = gy_copy(s, d, t, origin(at.y, ny, d, t - 1))
        copy.start()
        y_sent.append(copy)

    def across_copy(xh):
        return remote(c_ref, c_all.at[at.feat(xh, at.z, at.core)], gxs, gxr, across)

    def beside_copy(xl):
        return remote(x_ref, x_all.at[at.node(at.y, xl)], gls, glr, beside)

    across_copy(at.xh).start()
    beside_copy(at.xl).start()
    for d in (0, 1):
        z_start(0, d, 1)
        y_start(0, d, 1)
    sent_over = [sibling_copy(0, at.z, c_ref)]
    sent_over[0].start()
    def y_arrive(s, t):
        for d in (0, 1):
            if t <= last_y(s, d):
                gy_copy(s, d, t, origin(at.y, ny, d, t)).wait_recv()
                if t < last_y(s, d):
                    y_start(s, d, t + 1)

    def z_arrive(s, d, t):
        origin_z = origin(at.z, nz, d, t)
        gz_copy(s, d, t, origin_z).wait_recv()
        if t < last_z(s, d):
            z_start(s, d, t + 1)
        return sibling_copy(s, origin_z)

    ways = [(s, d) for s in (0, 1) for d in (0, 1)]

    def order(count):
        steps = [(0, 1), (0, 2)]
        for t in range(1, count + 1):
            steps += [(1, t), (0, t + 2)]
        return [(s, t) for s, t in steps if t <= count]

    z_order = [(s, d, t) for s, t in order(half_z) for d in (0, 1) if t <= last_z(s, d)]
    y_order = order(half_y)

    def z_next(count):
        over = [z_arrive(*z_order.pop(0)) for _ in range(min(count, len(z_order)))]
        for copy in over:
            copy.start()
        sent_over.extend(over)

    z_next(2)
    y_arrive(*y_order.pop(0))
    across_copy(1 - at.xh).wait_recv()
    for d in (0, 1):
        z_start(1, d, 1)
    partners = sibling_copy(1, at.z)
    partners.start()
    sent_over.append(partners)
    beside_copy(1 - at.xl).wait_recv()
    for d in (0, 1):
        y_start(1, d, 1)
    for load in loads:
        load.wait()
    spread_chains(rows, cols, live[0], n_feat, n_nodes, row_mat, col_mat, chain)
    chain_copy = pltpu.make_async_copy(chain.at[pl.ds(0, slots)], index, load_sem.at[0])
    chain_copy.start()
    while y_order:
        if len(y_order) > 1:
            z_next(2)
        y_arrive(*y_order.pop(0))

    def add_chain(sums, terms, before, k0):
        for u, term in enumerate(terms):
            prev = index[k0 + u, before]
            sums[k0 + u] = term + jnp.where(prev >= 0, sums[jnp.maximum(prev, 0)], 0.0)

    def ahead_step(g):
        terms = [
            jnp.dot(tiles[g * GROUP + u], x_all[cols[g * GROUP + u]], preferred_element_type=jnp.float32)
            for u in range(GROUP)
        ]
        add_chain(ahead, terms, 0, g * GROUP)

    def back_step(g):
        terms = [
            lax.dot_general(
                tiles[g * GROUP + u], c_all[rows[g * GROUP + u]], (((0,), (0,)), ((), ())),
                preferred_element_type=jnp.float32,
            )
            for u in range(GROUP)
        ]
        add_chain(back, terms, 1, g * GROUP)

    def own_p(xh, z, core):
        k = index[at.feat(xh, z, core), 2]
        return jnp.where(k >= 0, ahead[jnp.maximum(k, 0)], 0.0)

    def own_b(y, xl):
        k = index[at.node(y, xl), 3]
        return jnp.where(k >= 0, back[jnp.maximum(k, 0)], 0.0)

    groups = slots // GROUP
    tile_copy.wait()
    chain_copy.wait()
    parts = 2
    for part in range(parts):
        z_next(1)
        loop(groups * part // parts, groups * (part + 1) // parts, ahead_step)

    def c_copy(xh, z):
        slot = xh * nz + z
        return remote(p_tx.at[slot], c_rx.at[slot], cs.at[slot], cr.at[slot], sibling)

    def c_step(xh, z):
        p_tx[xh * nz + z] = own_p(xh, z, 1 - at.core).astype(jnp.bfloat16)
        c_copy(xh, z).start()

    for part in range(parts):
        first, end = nz * part // parts, nz * (part + 1) // parts
        loop(first, min(end, nz - 1), lambda t: c_step(1 - at.xh, z_peer(t)[0]))
        z_next(1)
    c_step(1 - at.xh, at.z)

    def x_copy(z):
        return remote(x_tx.at[z], x_rx.at[z], xs.at[z], xr.at[z], across)

    def x_step(z):
        c_copy(1 - at.xh, z).wait_recv()
        x_tx[z] = (own_p(1 - at.xh, z, at.core) + wide(c_rx[(1 - at.xh) * nz + z])).astype(jnp.bfloat16)
        x_copy(z).start()

    parts = len(z_order)
    for part in range(parts):
        first, end = nz * part // parts, nz * (part + 1) // parts
        loop(first, min(end, nz - 1), lambda t: x_step(z_peer(t)[0]))
        z_next(1)
    x_step(at.z)
    loop(0, nz - 1, lambda t: c_step(at.xh, z_peer(t)[0]))
    c_step(at.xh, at.z)

    for s in (0, 1):
        for z in range(nz):
            sibling_copy(s, z, arriving=True).wait_recv()
    loop(0, groups, back_step)

    def round_b(t):
        b_all[t] = own_b(lax.div(t, PAIR), lax.rem(t, PAIR)).astype(jnp.bfloat16)

    loop(0, n_nodes, round_b)
    width = x_all.shape[-1]
    term = lax.dot_general(
        x_all[...].reshape(-1, width), b_all[...].reshape(-1, width), (((0,), (0,)), ((), ())),
        preferred_element_type=jnp.float32,
    )
    w0[...] = term.astype(w0.dtype).reshape(w0.shape)

    def w1_copy(t):
        i, device = node_peer(t)
        return remote(w0.at[i], w1.at[at.i], w1s.at[i], w1r.at[at.i], device)

    loop(1, n_nodes, lambda t: w1_copy(t).start())

    def y_hops(d, s):
        return half_y if d == s else ny - 1 - half_y

    def ry_copy(d, s, h):
        return remote(ry_tx.at[d, s, h - 1], ry_rx.at[d, s, h - 1], rys.at[d, s, h - 1], ryr.at[d, s, h - 1], along_y[d])

    def y_hop(h):
        for d, s in ways:
            hops = y_hops(d, s)
            if h <= hops:
                value = own_b(origin(at.y, ny, 1 - d, hops + 1 - h), xl_of(s))
                if h > 1:
                    ry_copy(d, s, h - 1).wait_recv()
                    value = value + wide(ry_rx[d, s, h - 2])
                ry_tx[d, s, h - 1] = value.astype(jnp.bfloat16)
                ry_copy(d, s, h).start()

    def y_sum(s):
        value = own_b(at.y, xl_of(s))
        for d in (0, 1):
            hops = y_hops(d, s)
            ry_copy(d, s, hops).wait_recv()
            value = value + wide(ry_rx[d, s, hops - 1])
        return value

    z_hops = (half_z, nz - 1 - half_z)

    def rz_refs(d, h):
        late = h - (z_hops[d] - 1)
        return (rz_tx32.at[d, late], rz_rx32.at[d, late]) if late >= 0 else (rz_tx.at[d, h - 1], rz_rx.at[d, h - 1])

    def rz_copy(d, h):
        return remote(*rz_refs(d, h), rzs.at[d, h - 1], rzr.at[d, h - 1], along_z[d])

    def four_sum(z):
        c_copy(at.xh, z).wait_recv()
        x_copy(z).wait_recv()
        return own_p(at.xh, z, at.core) + wide(c_rx[at.xh * nz + z]) + wide(x_rx[z])

    def z_hop(h):
        for d in (0, 1):
            hops = z_hops[d]
            if h <= hops:
                value = four_sum(origin(at.z, nz, 1 - d, hops + 1 - h))
                if h > 1:
                    rz_copy(d, h - 1).wait_recv()
                    value = value + wide(rz_refs(d, h - 1)[1][...])
                tx = rz_refs(d, h)[0]
                tx[...] = value.astype(tx.dtype)
                rz_copy(d, h).start()

    y_hop(1)
    z_hop(1)
    z_hop(2)
    y_hop(2)
    z_hop(3)

    def w1_arrival(t):
        i, device = node_peer(t)
        remote(w0.at[i], w1.at[i], w1s.at[i], w1r.at[i], device).wait_recv()

    w1[at.i] = w0[at.i]
    loop(1, n_nodes, w1_arrival)
    me4 = at.xh * 2 + at.core
    w4[me4] = jnp.sum(wide(w1[...]), axis=0)
    four = [
        (at.xh * 2 + 1 - at.core, sibling),
        ((1 - at.xh) * 2 + at.core, across),
        ((1 - at.xh) * 2 + 1 - at.core, slanted),
    ]

    def w4_copy(slot, device):
        return remote(w4.at[me4], w4.at[me4], w4s.at[slot], w4r.at[me4], device)

    for slot, device in four:
        w4_copy(slot, device).start()
    z_hop(4)
    y_hop(3)

    for slot, device in four:
        remote(w4.at[slot], w4.at[slot], w4s.at[slot], w4r.at[slot], device).wait_recv()
    wz[at.z] = jnp.sum(w4[...], axis=0).astype(wz.dtype)

    def wz_copy(t):
        z, device = z_peer(t)
        return remote(wz.at[at.z], wz.at[at.z], wzs.at[z], wzr.at[at.z], device)

    loop(0, nz - 1, lambda t: wz_copy(t).start())
    z_hop(5)
    y_hop(4)
    z_hop(6)

    def wz_arrival(t):
        z, device = z_peer(t)
        remote(wz.at[z], wz.at[z], wzs.at[z], wzr.at[z], device).wait_recv()

    loop(0, nz - 1, wz_arrival)
    wn[at.i] = (jnp.sum(wide(wz[...]), axis=0) * scale).astype(wn.dtype)

    def wn_copy(t):
        i, device = node_peer(t)
        return remote(wn.at[at.i], wn.at[at.i], wns.at[i], wnr.at[at.i], device)

    loop(1, n_nodes, lambda t: wn_copy(t).start())

    for sent in sent_over + z_sent + y_sent:
        sent.wait_send()
    across_copy(at.xh).wait_send()
    beside_copy(at.xl).wait_send()
    for xh in (0, 1):
        loop(0, nz, lambda z: c_copy(xh, z).wait_send())
    loop(0, nz, lambda z: x_copy(z).wait_send())
    loop(1, n_nodes, lambda t: w1_copy(t).wait_send())
    l_copy = remote(l_tx, l_rx, ls, lr, beside)
    l_tx[...] = y_sum(1).astype(jnp.bfloat16)
    l_copy.start()
    near = y_sum(0)
    l_copy.wait_recv()
    fg_ref[...] = split_dot(near + wide(l_rx[...]), weight_ref[...], ((1,), (1,))).astype(fg_ref.dtype)

    whole = four_sum(at.z)
    for d in (0, 1):
        rz_copy(d, z_hops[d]).wait_recv()
        whole = whole + wide(rz_refs(d, z_hops[d])[1][...])
    out_ref[...] = split_dot(whole, weight_ref[...], ((1,), (0,))).astype(out_ref.dtype)

    def wn_arrival(t):
        i, device = node_peer(t)
        remote(wn.at[i], wn.at[i], wns.at[i], wnr.at[i], device).wait_recv()

    loop(1, n_nodes, wn_arrival)
    wg_ref[...] = wide(wn[...])

    for d, s in ways:
        for h in range(1, y_hops(d, s) + 1):
            ry_copy(d, s, h).wait_send()
    for d in (0, 1):
        for h in range(1, z_hops[d] + 1):
            rz_copy(d, h).wait_send()
    for slot, device in four:
        w4_copy(slot, device).wait_send()
    loop(0, nz - 1, lambda t: wz_copy(t).wait_send())
    l_copy.wait_send()
    loop(1, n_nodes, lambda t: wn_copy(t).wait_send())


def body(n_nodes, n_feat, features, weight, tiles, tile_rows, tile_cols, live, cotangent):
    rows, width = features.shape
    scale = 1.0 / math.sqrt(rows * n_nodes * n_feat)
    ny, nz = n_nodes // PAIR, n_feat // (PAIR * PAIR)
    slots, side = tiles.shape[:2]
    share = width // n_nodes
    dma = pltpu.SemaphoreType.DMA

    def blocks(*lead, kind=jnp.bfloat16):
        return pltpu.VMEM((*lead, rows, width), kind)

    def shares(count, kind):
        return pltpu.VMEM((count, share, width), kind)

    def pairs(*counts):
        return [sem for count in counts for sem in [dma(count) if count else dma] * 2]

    output, feature_grad, weight_grad = pl.pallas_call(
        functools.partial(kernel, n_nodes, n_feat, scale),
        out_shape=(
            jax.ShapeDtypeStruct((rows, width), jnp.bfloat16),
            jax.ShapeDtypeStruct((rows, width), jnp.bfloat16),
            jax.ShapeDtypeStruct((n_nodes, share, width), jnp.float32),
        ),
        in_specs=[ANY] * 7,
        out_specs=(VMEM,) * 3,
        scratch_shapes=[
            pltpu.SMEM(tile_rows.shape, jnp.int32),
            pltpu.SMEM(tile_cols.shape, jnp.int32),
            pltpu.SMEM(live.shape, jnp.int32),
            pltpu.VMEM((LANES, LANES), jnp.int32),
            pltpu.VMEM((LANES, LANES), jnp.int32),
            pltpu.VMEM((LANES, LANES), jnp.int32),
            pltpu.SMEM((slots, LANES), jnp.int32),
            pltpu.VMEM(weight.shape, weight.dtype),
            pltpu.VMEM(tiles.shape, tiles.dtype),
            blocks(n_nodes),
            blocks(n_feat),
            blocks(slots, kind=jnp.float32),
            blocks(slots, kind=jnp.float32),
            blocks(2 * nz),
            blocks(2 * nz),
            blocks(nz),
            blocks(nz),
            blocks(2, nz // 2),
            blocks(2, nz // 2),
            blocks(2, 2, kind=jnp.float32),
            blocks(2, 2, kind=jnp.float32),
            blocks(2, 2, ny // 2),
            blocks(2, 2, ny // 2),
            blocks(),
            blocks(),
            blocks(n_nodes),
            shares(n_nodes, jnp.bfloat16),
            shares(n_nodes, jnp.bfloat16),
            shares(4, jnp.float32),
            shares(nz, jnp.bfloat16),
            shares(n_nodes, jnp.bfloat16),
            dma((6,)),
            dma,
        ]
        + pairs(None, (2, 2, nz // 2), (2 * nz,), None, (2, 2, ny // 2))
        + pairs((2 * nz,), (nz,), (2, nz // 2), (2, 2, ny // 2), None)
        + pairs((n_nodes,), (4,), (nz,), (n_nodes,)),
        compiler_params=pltpu.CompilerParams(collective_id=0, has_side_effects=True, vmem_limit_bytes=LIMIT),
        name="graph_layer",
    )(tile_rows, tile_cols, live, features, cotangent, weight, tiles)
    return output, feature_grad, weight_grad.reshape(weight.shape)


def solution(mesh):
    in_specs = (
        P(("feat", "nodes"), None),
        P(),
        P(("nodes", "feat"), None, None),
        P(("nodes", "feat")),
        P(("nodes", "feat")),
        P(("nodes", "feat")),
        P(("nodes", "feat"), None),
    )
    out_specs = (P(("nodes", "feat"), None), P(("feat", "nodes"), None), P())
    step = functools.partial(body, mesh.shape["nodes"], mesh.shape["feat"])
    return jax.shard_map(step, mesh=mesh, in_specs=in_specs, out_specs=out_specs, check_vma=False)
```
